32 devices in a mesh: chan: 16 (over z, x, core), win: 2 (over y).
Axes of the slice: x: 2, y: 2, z: 4, core: 2. Of those that a mesh axis runs over, the one named last changes fastest.
Arguments:
- records: bfloat16 [8, 8192, 512], P('win', 'chan'), may hold values from -6 to 6
- block_pairs: int32 [512, 2], P('chan'), may hold values from 0 to 63, as said below
- lag_low: int32 [512], P('chan'), may hold values from 0 to 31
- lag_high: int32 [512], P('chan'), may hold values from 97 to 128
- slot_count: int32 [16], P('chan'), may hold values from 1 to 32, as said below
Outputs:
- stacks: float32 [512, 128, 128], P(('chan', 'win'))
The draws below stay inside these ranges and needn't reach their ends.
Inputs may be any that keep to these rules, and one draw needn't show every extreme that they name: `block_pairs`: slot p belongs to owner p // 32; for owner o both blocks of each slot lie within o * 4 - 16 to o * 4 + 19, and the two blocks differ by at most 16. Slots of owner o at or after slot_count[o] are unused; some owner uses all 32.
All inputs are finite; a program needn't handle non-finite values.
Results may differ from the reference program's by a relative error of at most 0.0015.
Values may be sent and summed in bfloat16 or wider, within the bound.
No kernel may reach another device: no remote copies, remote signals or barrier semaphores. Data moves between devices by JAX's collectives and lax.ppermute only.
A program may use at most 128 MiB of HBM per device.

```python
import math
import jax
import jax.numpy as jnp
from jax import lax

BLOCK = 128
NT = 512
F = 128
LAGS = 128
REACH = 16
B_DEV = 4
PO = 32
NB = 64
CHANNELS = 8192
NSEG = 8
NPAIRS = 512
N_CHAN = 16


def draw_block_pairs(key, part):
    key_first, key_second = jax.random.split(jax.random.fold_in(key, 11))
    owner = jnp.arange(NPAIRS, dtype=jnp.int32) // PO
    low = jnp.maximum(owner * B_DEV - REACH, 0)
    high = jnp.minimum(owner * B_DEV + B_DEV + REACH, NB) - 1
    first = owner * B_DEV + jax.random.randint(key_first, (NPAIRS,), -REACH, B_DEV + REACH)
    first = jnp.clip(first, low, high)
    second = first + jax.random.randint(key_second, (NPAIRS,), -REACH, REACH + 1)
    second = jnp.clip(second, low, high)
    return jnp.stack([first, second], axis=1).astype(jnp.int32)


def draw_slot_count(key, part):
    key_count, key_spot = jax.random.split(jax.random.fold_in(key, 23))
    counts = jax.random.randint(key_count, (N_CHAN,), 1, PO + 1)
    spot = jax.random.randint(key_spot, (), 0, N_CHAN)
    return jnp.where(jnp.arange(N_CHAN) == spot, PO, counts).astype(jnp.int32)


def with_ends(array, rng, low, top_value):
    longest = array.shape.index(max(array.shape))
    spots = []
    for shift in (0, 1):
        where = [jax.random.randint(jax.random.fold_in(rng, axis), (), 0, length) for axis, length in enumerate(array.shape)]
        where[longest] = (where[longest] + shift) % array.shape[longest]
        spots.append(tuple(where))
    return array.at[spots[0]].set(low).at[spots[1]].set(top_value)


def levels(own_key, dims, pieces, least, largest):
    def one(dim, parts):
        steps = jax.random.uniform(jax.random.fold_in(jax.random.fold_in(own_key, 6), dim), (parts,), jnp.float32, least / len(pieces), largest / len(pieces))
        return jnp.repeat(jnp.exp(steps), dims[dim] // parts).reshape((-1,) + (1,) * (len(dims) - dim - 1))

    factor_of = one(*pieces[0])
    for cut in pieces[1:]:
        factor_of = factor_of * one(*cut)
    return factor_of


def bell_draw(rng, dims, deviation, most, shards=(), held_as=jnp.bfloat16):
    drawn = jax.random.normal(rng, dims, jnp.float32) * deviation
    if len(shards) > 0:
        drawn = levels(rng, dims, shards, -0.22, 0.18) * drawn
    return jnp.clip(drawn, min=-most, max=most).astype(held_as)


def setup_inputs(seed: int = 0) -> dict:
    arg_keys = jax.random.split(jax.random.key(seed), 6)
    return {
        "records": bell_draw(arg_keys[0], (NSEG, CHANNELS, NT), 1.0, 6.0, ((0, 2), (1, 16))),
        "block_pairs": draw_block_pairs(jax.random.fold_in(arg_keys[5], 71), 0),
        "lag_low": with_ends(jax.random.randint(arg_keys[2], (NPAIRS,), 0, LAGS // 4), jax.random.fold_in(arg_keys[2], 1), 0, (LAGS // 4) - 1).astype(jnp.int32),
        "lag_high": with_ends(jax.random.randint(arg_keys[3], (NPAIRS,), 3 * LAGS // 4 + 1, LAGS + 1), jax.random.fold_in(arg_keys[3], 1), 3 * LAGS // 4 + 1, LAGS).astype(jnp.int32),
        "slot_count": draw_slot_count(jax.random.fold_in(arg_keys[5], 71), 0),
    }


def forward_table(length, bins):
    first = length // 32
    times = jnp.arange(length, dtype=jnp.int32)[:, None]
    freqs = (first + jnp.arange(bins, dtype=jnp.int32))[None, :]
    phase = 2.0 * math.pi / length * (times * freqs % length).astype(jnp.float32)
    return jnp.concatenate([jnp.cos(phase), -jnp.sin(phase)], axis=1).astype(jnp.bfloat16)

def inverse_table(length, bins, lag_total):
    first = length // 32
    freqs = (first + jnp.arange(bins, dtype=jnp.int32))[:, None]
    shifts = (jnp.arange(lag_total, dtype=jnp.int32) - lag_total // 2)[None, :]
    phase = 2.0 * math.pi / length * (freqs * shifts % length).astype(jnp.float32)
    return jnp.concatenate([jnp.cos(phase), -jnp.sin(phase)], axis=0)

def whiten(spectra, bins):
    real_part = spectra[..., :bins]
    imag_part = spectra[..., bins:]
    power = real_part * real_part + imag_part * imag_part
    level = lax.optimization_barrier(jnp.mean(power, axis=-1, keepdims=True))
    factor = lax.rsqrt(power + 0.1 * level + 1e-06)
    return jnp.concatenate([real_part * factor, imag_part * factor], axis=-1).astype(jnp.bfloat16)

def cross_spectrum(first, second, bins, seg_axis):
    first = first.astype(jnp.float32)
    second = second.astype(jnp.float32)
    first_re, first_im = (first[..., :bins], first[..., bins:])
    second_re, second_im = (second[..., :bins], second[..., bins:])
    real_sum = lax.optimization_barrier(jnp.sum(first_re * second_re + first_im * second_im, axis=seg_axis))
    imag_sum = lax.optimization_barrier(jnp.sum(first_re * second_im - first_im * second_re, axis=seg_axis))
    return jnp.concatenate([real_sum, imag_sum], axis=-1)

def reference(records, block_pairs, lag_low, lag_high, slot_count):
    forward = forward_table(NT, F)

    def transform(segment):
        return whiten(jnp.dot(segment, forward, preferred_element_type=jnp.float32), F)
    whitened = lax.map(transform, records)
    inverse = inverse_table(NT, F, LAGS)
    factor = 1.0 / math.sqrt(F * NSEG)
    lag_index = jnp.arange(LAGS, dtype=jnp.int32)

    def one_pair(index):
        first = lax.dynamic_slice_in_dim(whitened, (block_pairs[index, 0] * BLOCK).astype(jnp.int32), BLOCK, 1)
        second = lax.dynamic_slice_in_dim(whitened, (block_pairs[index, 1] * BLOCK).astype(jnp.int32), BLOCK, 1)
        spectrum = cross_spectrum(first, second, F, 0)
        stack = jnp.dot(spectrum, inverse, precision=lax.Precision.HIGHEST, preferred_element_type=jnp.float32) * factor
        used = index % PO < slot_count[index // PO]
        keep = (lag_index >= lag_low[index]) & (lag_index < lag_high[index]) & used
        return jnp.where(keep[None, :], stack, jnp.zeros_like(stack))
    return lax.map(one_pair, jnp.arange(NPAIRS, dtype=jnp.int32))
```

```python
import functools
import math

import jax
import jax.numpy as jnp
import numpy as np
from jax import lax
from jax.experimental import pallas as pl
from jax.experimental.pallas import tpu as pltpu
from jax.sharding import PartitionSpec as P

BLOCK = 128
F = 128
LAGS = 128
REACH = 16
VMEM_LIMIT = 48 * 1024 * 1024


def forward_table(length):
    first = length // 32
    times = np.arange(length, dtype=np.int64)[:, None]
    freqs = (first + np.arange(F, dtype=np.int64))[None, :]
    phase = 2.0 * math.pi / length * (times * freqs % length)
    table = np.concatenate([np.cos(phase), -np.sin(phase)], axis=1)
    return jnp.asarray(table.astype(np.float32)).astype(jnp.bfloat16)


def inverse_tables(length, factor):
    first = length // 32
    freqs = (first + np.arange(F, dtype=np.int64))[:, None]
    shifts = (np.arange(LAGS, dtype=np.int64) - LAGS // 2)[None, :]
    phase = 2.0 * math.pi / length * (freqs * shifts % length)
    table = (np.concatenate([np.cos(phase), -np.sin(phase)], axis=0) * factor).astype(np.float32)
    high = table.astype(jnp.bfloat16)
    low = (table - high.astype(np.float32)).astype(jnp.bfloat16)
    return jnp.asarray(np.concatenate([high, low], axis=1))


def spectra_kernel(parts, records_ref, table_ref, out_ref):
    blocks = out_ref.shape[1]
    for block in range(blocks):
        rows = records_ref[0, pl.ds(block * BLOCK, BLOCK), :]
        spectra = jnp.dot(rows, table_ref[...], preferred_element_type=jnp.float32)
        real_part, imag_part = spectra[:, :F], spectra[:, F:]
        power = real_part * real_part + imag_part * imag_part
        level = jnp.mean(power, axis=-1, keepdims=True)
        scale = lax.rsqrt(power + 0.1 * level + 1e-06)
        whitened = jnp.concatenate([real_part * scale, imag_part * scale], axis=1)
        out_ref[:, block] = whitened.astype(jnp.bfloat16).reshape(parts, BLOCK // parts, 2 * F)


def whitened_parts(records, parts):
    segments, channels, length = records.shape
    blocks, width = channels // BLOCK, BLOCK // parts
    packed = width % 16 == 0
    cut = parts if packed else 1
    whitened = pl.pallas_call(
        functools.partial(spectra_kernel, cut),
        grid=(segments,),
        in_specs=[
            pl.BlockSpec((1, channels, length), lambda s: (s, 0, 0)),
            pl.BlockSpec((length, 2 * F), lambda s: (0, 0)),
        ],
        out_specs=pl.BlockSpec((cut, blocks, BLOCK // cut, 2 * F), lambda s: (0, 0, s, 0)),
        out_shape=jax.ShapeDtypeStruct(
            (cut, blocks, segments * BLOCK // cut, 2 * F), jnp.bfloat16
        ),
        compiler_params=pltpu.CompilerParams(vmem_limit_bytes=VMEM_LIMIT),
    )(records, forward_table(length))
    if packed:
        return whitened
    whitened = whitened.reshape(blocks, segments, parts, width, 2 * F)
    return whitened.transpose(2, 0, 1, 3, 4).reshape(parts, blocks, segments * width, 2 * F)


def pair_kernel(step, wins, pairs_ref, counts_ref, below, own, above, table_ref, out_ref, held, cross, sem):
    parts, blocks = own.shape[:2]
    copies = [pltpu.make_async_copy(ref, held.at[k], sem.at[k]) for k, ref in enumerate((below, own, above))]
    for copy in copies:
        copy.start()
    for copy in copies:
        copy.wait()
    slots = out_ref.shape[1] // step
    rows = own.shape[2]
    owned = parts // wins * blocks

    def place(block):
        group, rest = block // owned, block % owned
        return group, rest // blocks, rest % blocks

    def part_of(part, _):
        owner, win = part // wins, part % wins

        def one_pair(slot, _):
            pair = part * slots + slot
            ga, ja, ba = place(pairs_ref[2 * pair])
            gb, jb, bb = place(pairs_ref[2 * pair + 1])
            real_sum = jnp.zeros((step, F), jnp.float32)
            imag_sum = jnp.zeros((step, F), jnp.float32)
            for w in range(wins):
                for r in range(0, rows, step):
                    a = held[ga, ja * wins + w, ba, pl.ds(r, step), :].astype(jnp.float32)
                    b = held[gb, jb * wins + w, bb, pl.ds(r, step), :].astype(jnp.float32)
                    ar, ai, br, bi = a[:, :F], a[:, F:], b[:, :F], b[:, F:]
                    real_sum += ar * br + ai * bi
                    imag_sum += ar * bi - ai * br
            cross[pl.ds(pl.multiple_of(slot * step, step), step), pl.ds(0, F)] = real_sum
            cross[pl.ds(pl.multiple_of(slot * step, step), step), pl.ds(F, F)] = imag_sum
            return 0

        count = jnp.clip(counts_ref[owner] - win * slots, 0, slots)
        lax.fori_loop(0, count, one_pair, 0)
        spectrum = cross[...]
        high = spectrum.astype(jnp.bfloat16)
        low = (spectrum - high.astype(jnp.float32)).astype(jnp.bfloat16)
        first = jnp.dot(high, table_ref[...], preferred_element_type=jnp.float32)
        second = jnp.dot(low, table_ref[:, :LAGS], preferred_element_type=jnp.float32)
        out_ref[part] = first[:, :LAGS] + (first[:, LAGS:] + second)
        return 0

    lax.fori_loop(0, parts, part_of, 0)


def per_device(records, block_pairs, lag_low, lag_high, slot_count):
    segments, channels, length = records.shape
    blocks = channels // BLOCK
    chans, wins = lax.axis_size("chan"), lax.axis_size("win")
    near = REACH // blocks
    parts = near * wins
    width = BLOCK // parts
    slots = block_pairs.shape[0]
    share = slots // wins
    groups = [[q * parts + k for k in range(parts)] for q in range(chans // near)]
    exchange = functools.partial(
        lax.all_to_all,
        axis_name=("chan", "win"),
        split_axis=0,
        concat_axis=0,
        axis_index_groups=groups,
        tiled=True,
    )

    own = exchange(whitened_parts(records, parts))
    win = lax.axis_index("win")
    base = (lax.axis_index("chan") // near - 1) * REACH
    local = jnp.clip(block_pairs - base, 0, 3 * REACH - 1)
    mine = lax.dynamic_slice_in_dim(local, win * share, share).reshape(2 * share)
    note = jnp.concatenate([mine, slot_count, jnp.zeros(128 - 2 * share - 1, jnp.int32)])
    notes = exchange(jnp.broadcast_to(note, (parts, 128)))
    pairs = notes[:, : 2 * share].reshape(parts * 2 * share)
    counts = notes[:: wins, 2 * share]

    up = [(i, i + near) for i in range(chans - near)]
    below = lax.ppermute(own, "chan", up)
    above = lax.ppermute(own, "chan", [(b, a) for a, b in up])

    step = max(width, 16)
    factor = 1.0 / math.sqrt(F * segments * wins)
    hbm = pl.BlockSpec(memory_space=pl.ANY)
    smem = pl.BlockSpec(memory_space=pltpu.SMEM)
    vmem = pl.BlockSpec(memory_space=pltpu.VMEM)
    lagged = pl.pallas_call(
        functools.partial(pair_kernel, step, wins),
        in_specs=[smem, smem, hbm, hbm, hbm, vmem],
        out_specs=vmem,
        out_shape=jax.ShapeDtypeStruct((parts, share * step, LAGS), jnp.float32),
        scratch_shapes=[
            pltpu.VMEM((3,) + own.shape, jnp.bfloat16),
            pltpu.VMEM((share * step, 2 * F), jnp.float32),
            pltpu.SemaphoreType.DMA((3,)),
        ],
        compiler_params=pltpu.CompilerParams(vmem_limit_bytes=VMEM_LIMIT),
    )(pairs, counts, below, own, above, inverse_tables(length, factor))

    if step > width:
        lagged = lagged.reshape(parts, share, step // width, width, LAGS).sum(axis=2)
    stack = exchange(lagged).reshape(parts, share, width, LAGS)
    stack = stack.transpose(1, 0, 2, 3).reshape(share, BLOCK, LAGS)
    start = win * share
    low = lax.dynamic_slice_in_dim(lag_low, start, share)
    high = lax.dynamic_slice_in_dim(lag_high, start, share)
    lag_index = jnp.arange(LAGS, dtype=jnp.int32)[None, :]
    used = start + jnp.arange(share, dtype=jnp.int32) < slot_count[0]
    keep = (lag_index >= low[:, None]) & (lag_index < high[:, None]) & used[:, None]
    return jnp.where(keep[:, None, :], stack, jnp.zeros_like(stack))


def solution(mesh):
    in_specs = (P("win", "chan", None), P("chan", None), P("chan"), P("chan"), P("chan"))
    out_specs = P(("chan", "win"), None, None)
    return jax.shard_map(
        per_device, mesh=mesh, in_specs=in_specs, out_specs=out_specs, check_vma=False
    )
```

```python
import functools
import math

import jax
import jax.numpy as jnp
import numpy as np
from jax import lax
from jax.experimental import pallas as pl
from jax.experimental.pallas import tpu as pltpu
from jax.sharding import PartitionSpec as P

BLOCK = 128
F = 128
LAGS = 128
REACH = 16
VMEM_LIMIT = 48 * 1024 * 1024


def forward_table(length):
    first = length // 32
    times = np.arange(length, dtype=np.int64)[:, None]
    freqs = (first + np.arange(F, dtype=np.int64))[None, :]
    phase = 2.0 * math.pi / length * (times * freqs % length)
    table = np.concatenate([np.cos(phase), -np.sin(phase)], axis=1)
    return jnp.asarray(table.astype(np.float32)).astype(jnp.bfloat16)


def inverse_tables(length, factor):
    first = length // 32
    freqs = (first + np.arange(F, dtype=np.int64))[:, None]
    shifts = (np.arange(LAGS, dtype=np.int64) - LAGS // 2)[None, :]
    phase = 2.0 * math.pi / length * (freqs * shifts % length)
    table = (np.concatenate([np.cos(phase), -np.sin(phase)], axis=0) * factor).astype(np.float32)
    high = table.astype(jnp.bfloat16)
    low = (table - high.astype(np.float32)).astype(jnp.bfloat16)
    return jnp.asarray(np.concatenate([high, low], axis=1))


def spectra_kernel(parts, chunks, records_ref, table_ref, *out_refs):
    segments = records_ref.shape[0]
    blocks = out_refs[0].shape[1]
    span = BLOCK // chunks
    for block in range(blocks):
        held = []
        for segment in range(segments):
            rows = records_ref[segment, pl.ds(block * BLOCK, BLOCK), :]
            spectra = jnp.dot(rows, table_ref[...], preferred_element_type=jnp.float32)
            real_part, imag_part = spectra[:, :F], spectra[:, F:]
            power = real_part * real_part + imag_part * imag_part
            level = jnp.mean(power, axis=-1, keepdims=True)
            scale = lax.rsqrt(power + 0.1 * level + 1e-06)
            held.append(jnp.concatenate([real_part * scale, imag_part * scale], axis=1))
        for chunk, out_ref in enumerate(out_refs):
            pieces = [
                whitened[chunk * span : (chunk + 1) * span].reshape(parts, span // parts, 2 * F)
                for whitened in held
            ]
            out_ref[:, block] = jnp.concatenate(pieces, axis=1).astype(jnp.bfloat16)


def whitened_parts(records, parts, chunks):
    segments, channels, length = records.shape
    blocks, width = channels // BLOCK, BLOCK // parts // chunks
    packed = width % 8 == 0
    cut = parts if packed else 1
    together = 2
    outs = pl.pallas_call(
        functools.partial(spectra_kernel, cut, chunks),
        grid=(segments // together,),
        in_specs=[
            pl.BlockSpec((together, channels, length), lambda s: (s, 0, 0)),
            pl.BlockSpec((length, 2 * F), lambda s: (0, 0)),
        ],
        out_specs=[
            pl.BlockSpec(
                (cut, blocks, together * BLOCK // cut // chunks, 2 * F), lambda s: (0, 0, s, 0)
            )
        ]
        * chunks,
        out_shape=[
            jax.ShapeDtypeStruct(
                (cut, blocks, segments * BLOCK // cut // chunks, 2 * F), jnp.bfloat16
            )
        ]
        * chunks,
        compiler_params=pltpu.CompilerParams(vmem_limit_bytes=VMEM_LIMIT),
    )(records, forward_table(length))
    if packed:
        return outs
    return [
        out.reshape(blocks, segments, parts, width, 2 * F)
        .transpose(2, 0, 1, 3, 4)
        .reshape(parts, blocks, segments * width, 2 * F)
        for out in outs
    ]


def pair_kernel(fold, wins, pairs_ref, counts_ref, below, own, above, table_ref, out_ref, held, cross, sem):
    parts, blocks = own.shape[:2]
    copies = [
        pltpu.make_async_copy(ref, held.at[k], sem.at[k])
        for k, ref in enumerate((below, own, above))
    ]
    for copy in copies:
        copy.start()
    for copy in copies:
        copy.wait()
    slots = out_ref.shape[1] // fold
    rows = own.shape[2]
    owned = parts // wins * blocks

    def place(block):
        group, rest = block // owned, block % owned
        return group, rest // blocks, rest % blocks

    def part_of(part, _):
        owner, win = part // wins, part % wins

        def one_pair(slot, _):
            pair = part * slots + slot
            ga, ja, ba = place(pairs_ref[2 * pair])
            gb, jb, bb = place(pairs_ref[2 * pair + 1])
            real_sum = jnp.zeros((16, F), jnp.float32)
            imag_sum = jnp.zeros((16, F), jnp.float32)
            for w in range(wins):
                for r in range(0, rows, 16):
                    a = held[ga, ja * wins + w, ba, pl.ds(r, 16), :].astype(jnp.float32)
                    b = held[gb, jb * wins + w, bb, pl.ds(r, 16), :].astype(jnp.float32)
                    ar, ai, br, bi = a[:, :F], a[:, F:], b[:, :F], b[:, F:]
                    real_sum += ar * br + ai * bi
                    imag_sum += ar * bi - ai * br
            if fold == 8:
                real_sum = real_sum[:8] + real_sum[8:]
                imag_sum = imag_sum[:8] + imag_sum[8:]
            spot = pl.ds(pl.multiple_of(slot * fold, fold), fold)
            cross[spot, pl.ds(0, F)] = real_sum
            cross[spot, pl.ds(F, F)] = imag_sum
            return 0

        count = jnp.clip(counts_ref[owner] - win * slots, 0, slots)
        lax.fori_loop(0, count, one_pair, 0)
        spectrum = cross[...]
        high = spectrum.astype(jnp.bfloat16)
        low = (spectrum - high.astype(jnp.float32)).astype(jnp.bfloat16)
        first = jnp.dot(high, table_ref[...], preferred_element_type=jnp.float32)
        second = jnp.dot(low, table_ref[:, :LAGS], preferred_element_type=jnp.float32)
        out_ref[part] = first[:, :LAGS] + (first[:, LAGS:] + second)
        return 0

    lax.fori_loop(0, parts, part_of, 0)


def pair_stacks(pairs, counts, below, own, above, table, share, width, wins):
    parts = own.shape[0]
    fold = 16 if width % 16 == 0 else 8
    hbm = pl.BlockSpec(memory_space=pl.ANY)
    smem = pl.BlockSpec(memory_space=pltpu.SMEM)
    vmem = pl.BlockSpec(memory_space=pltpu.VMEM)
    lagged = pl.pallas_call(
        functools.partial(pair_kernel, fold, wins),
        in_specs=[smem, smem, hbm, hbm, hbm, vmem],
        out_specs=vmem,
        out_shape=jax.ShapeDtypeStruct((parts, share * fold, LAGS), jnp.float32),
        scratch_shapes=[
            pltpu.VMEM((3,) + own.shape, jnp.bfloat16),
            pltpu.VMEM((share * fold, 2 * F), jnp.float32),
            pltpu.SemaphoreType.DMA((3,)),
        ],
        compiler_params=pltpu.CompilerParams(vmem_limit_bytes=VMEM_LIMIT),
    )(pairs, counts, below, own, above, table)
    if fold > width:
        lagged = lagged.reshape(parts, share, fold // width, width, LAGS).sum(axis=2)
    return lagged.reshape(parts, share, width, LAGS)


def per_device(records, block_pairs, lag_low, lag_high, slot_count):
    segments, channels, length = records.shape
    blocks = channels // BLOCK
    chans, wins = lax.axis_size("chan"), lax.axis_size("win")
    near = REACH // blocks
    parts = near * wins
    slots = block_pairs.shape[0]
    share = slots // wins
    groups = [[q * parts + k for k in range(parts)] for q in range(chans // near)]
    exchange = functools.partial(
        lax.all_to_all,
        axis_name=("chan", "win"),
        split_axis=0,
        concat_axis=0,
        axis_index_groups=groups,
        tiled=True,
    )

    chunks = max(1, min(2, BLOCK // parts // 8))
    width = BLOCK // parts // chunks
    up = [(i, i + near) for i in range(chans - near)]
    down = [(b, a) for a, b in up]
    planes = []
    for piece in whitened_parts(records, parts, chunks):
        own = exchange(piece)
        planes.append((lax.ppermute(own, "chan", up), own, lax.ppermute(own, "chan", down)))

    win = lax.axis_index("win")
    base = (lax.axis_index("chan") // near - 1) * REACH
    local = jnp.clip(block_pairs - base, 0, 3 * REACH - 1)
    mine = lax.dynamic_slice_in_dim(local, win * share, share).reshape(2 * share)
    note = jnp.concatenate([mine, slot_count, jnp.zeros(128 - 2 * share - 1, jnp.int32)])
    notes = exchange(jnp.broadcast_to(note, (parts, 128)))
    pairs = notes[:, : 2 * share].reshape(parts * 2 * share)
    counts = notes[:: wins, 2 * share]

    table = inverse_tables(length, 1.0 / math.sqrt(F * segments * wins))
    lagged = [
        exchange(pair_stacks(pairs, counts, *plane, table, share, width, wins)) for plane in planes
    ]
    stack = jnp.stack(lagged).transpose(2, 0, 1, 3, 4).reshape(share, BLOCK, LAGS)
    start = win * share
    low = lax.dynamic_slice_in_dim(lag_low, start, share)
    high = lax.dynamic_slice_in_dim(lag_high, start, share)
    lag_index = jnp.arange(LAGS, dtype=jnp.int32)[None, :]
    used = start + jnp.arange(share, dtype=jnp.int32) < slot_count[0]
    keep = (lag_index >= low[:, None]) & (lag_index < high[:, None]) & used[:, None]
    return jnp.where(keep[:, None, :], stack, jnp.zeros_like(stack))


def solution(mesh):
    in_specs = (P("win", "chan", None), P("chan", None), P("chan"), P("chan"), P("chan"))
    out_specs = P(("chan", "win"), None, None)
    return jax.shard_map(
        per_device, mesh=mesh, in_specs=in_specs, out_specs=out_specs, check_vma=False
    )
```

```python
import functools
import math

import jax
import jax.numpy as jnp
import numpy as np
from jax import lax
from jax.experimental import pallas as pl
from jax.experimental.pallas import tpu as pltpu
from jax.sharding import PartitionSpec as P

BLOCK = 128
F = 128
LAGS = 128
REACH = 16
NOTE_ROWS = 16
VMEM_LIMIT = 48 * 1024 * 1024


def forward_table(length):
    first = length // 32
    times = np.arange(length, dtype=np.int64)[:, None]
    freqs = (first + np.arange(F, dtype=np.int64))[None, :]
    phase = 2.0 * math.pi / length * (times * freqs % length)
    table = np.concatenate([np.cos(phase), -np.sin(phase)], axis=1)
    return jnp.asarray(table.astype(np.float32)).astype(jnp.bfloat16)


def inverse_tables(length, factor):
    first = length // 32
    freqs = (first + np.arange(F, dtype=np.int64))[:, None]
    shifts = (np.arange(LAGS, dtype=np.int64) - LAGS // 2)[None, :]
    phase = 2.0 * math.pi / length * (freqs * shifts % length)
    table = (np.concatenate([np.cos(phase), -np.sin(phase)], axis=0) * factor).astype(np.float32)
    high = table.astype(jnp.bfloat16)
    low = (table - high.astype(np.float32)).astype(jnp.bfloat16)
    return jnp.asarray(np.concatenate([high, low], axis=1))


def encode(values):
    values = values * jnp.abs(values)
    return (values * jnp.abs(values)).astype(jnp.bfloat16)


def decode(code, scale):
    code = code.astype(jnp.float32)
    root = jnp.sqrt(jnp.sqrt(jnp.abs(code))) * scale
    return jnp.where(code < 0, -root, root)


def spectra_kernel(near, wins, records, pairs_ref, count_ref, table_ref, out_ref, held, note, sem):
    segments, channels, _ = records.shape
    cut, blocks = out_ref.shape[0], channels // BLOCK
    width = BLOCK // cut
    chan = lax.axis_index("chan")
    mine = lax.rem(chan, near) * wins + lax.axis_index("win")
    copies = [
        pltpu.make_async_copy(records.at[s], held.at[s], sem.at[s]) for s in range(segments)
    ]
    for copy in copies:
        copy.start()
    base = (lax.div(chan, near) - 1) * REACH
    slots = pairs_ref.shape[1]
    note[...] = jnp.zeros_like(note)
    note[0:2, 0:slots] = jnp.clip(pairs_ref[...] - base, 0, 3 * REACH - 1).astype(jnp.float32)
    note[2:3, :] = jnp.full((1, note.shape[1]), count_ref[0], jnp.int32).astype(jnp.float32)
    notes = note[...].astype(jnp.bfloat16)
    for part in range(cut):
        out_ref[part, pl.ds(out_ref.shape[1] - NOTE_ROWS, NOTE_ROWS), :] = notes
    for s in range(segments):
        copies[s].wait()
        for block in range(blocks):
            rows = held[s, pl.ds(block * BLOCK, BLOCK), :]
            spectra = jnp.dot(rows, table_ref[...], preferred_element_type=jnp.float32)
            real_part, imag_part = spectra[:, :F], spectra[:, F:]
            power = real_part * real_part + imag_part * imag_part
            level = jnp.mean(power, axis=-1, keepdims=True)
            scale = lax.rsqrt(power + 0.1 * level + 1e-06)
            whitened = jnp.concatenate([real_part * scale, imag_part * scale], axis=1)
            whitened = whitened.astype(jnp.bfloat16)
            spot = pl.ds((block * segments + s) * width, width)
            if cut == 1:
                out_ref[0, spot, :] = whitened
            else:
                for part in range(cut):
                    piece = whitened[part * width : (part + 1) * width]
                    out_ref[jnp.bitwise_xor(mine, part), spot, :] = piece


def whitened_parts(records, block_pairs, slot_count, near, wins):
    segments, channels, length = records.shape
    blocks, parts = channels // BLOCK, near * wins
    width = BLOCK // parts
    packed = width % 16 == 0
    cut = parts if packed else 1
    rows = blocks * segments * BLOCK // cut
    hbm = pl.BlockSpec(memory_space=pl.ANY)
    vmem = pl.BlockSpec(memory_space=pltpu.VMEM)
    smem = pl.BlockSpec(memory_space=pltpu.SMEM)
    out = pl.pallas_call(
        functools.partial(spectra_kernel, near, wins),
        in_specs=[hbm, vmem, smem, vmem],
        out_specs=vmem,
        out_shape=jax.ShapeDtypeStruct((cut, rows + NOTE_ROWS, 2 * F), jnp.bfloat16),
        scratch_shapes=[
            pltpu.VMEM(records.shape, jnp.bfloat16),
            pltpu.VMEM((NOTE_ROWS, 2 * F), jnp.float32),
            pltpu.SemaphoreType.DMA((segments,)),
        ],
        compiler_params=pltpu.CompilerParams(vmem_limit_bytes=VMEM_LIMIT),
    )(records, block_pairs.T, slot_count, forward_table(length))
    if packed:
        return out
    mine = lax.axis_index("chan") % near * wins + lax.axis_index("win")
    split = out[0, :rows].reshape(blocks, segments, parts, width, 2 * F)
    split = split.transpose(2, 0, 1, 3, 4).reshape(parts, blocks * segments * width, 2 * F)
    split = jnp.take(split, jnp.bitwise_xor(mine, jnp.arange(parts)), axis=0)
    notes = jnp.broadcast_to(out[0, rows:], (parts, NOTE_ROWS, 2 * F))
    return jnp.concatenate([split, notes], axis=1)


def pair_kernel(near, wins, fold, firsts, seconds, counts, table_ref, *refs):
    chips = near // 2 * wins
    pieces, (out_ref, held, cross, sem) = refs[: 3 * chips], refs[3 * chips :]
    size = held.shape[0] // (3 * chips)
    copies = [
        pltpu.make_async_copy(
            piece.at[pl.ds(0, size)], held.at[pl.ds(k * size, size)], sem.at[k]
        )
        for k, piece in enumerate(pieces)
    ]
    for copy in copies:
        copy.start()
    for copy in copies:
        copy.wait()
    slots = cross.shape[0] // fold
    together = min(4, slots)
    plane = near // 2 * size
    rows = plane // REACH
    mine = lax.rem(lax.axis_index("chan"), near)

    def one_pair(owner, win, slot):
        index = owner * (slots * wins) + win * slots + slot
        first, second = firsts[index], seconds[index]
        real_sum = jnp.zeros((16, F), jnp.float32)
        imag_sum = jnp.zeros((16, F), jnp.float32)
        for w in range(wins):
            for r in range(0, rows, 16):
                a = held[pl.ds(pl.multiple_of(first + (w * plane + r), 16), 16), :]
                b = held[pl.ds(pl.multiple_of(second + (w * plane + r), 16), 16), :]
                a, b = a.astype(jnp.float32), b.astype(jnp.float32)
                ar, ai, br, bi = a[:, :F], a[:, F:], b[:, :F], b[:, F:]
                real_sum += ar * br + ai * bi
                imag_sum += ar * bi - ai * br
        spot = pl.ds(pl.multiple_of(slot * fold, fold), fold)
        cross[spot, pl.ds(0, F)] = real_sum
        cross[spot, pl.ds(F, F)] = imag_sum

    def part_of(part, _):
        owner, win = lax.div(part, wins), lax.rem(part, wins)

        def some_pairs(step, _):
            for k in range(together):
                one_pair(owner, win, step * together + k)
            return 0

        count = jnp.clip(counts[owner] - win * slots, 0, slots)
        lax.fori_loop(0, lax.div(count + (together - 1), together), some_pairs, 0)
        spectrum = cross[...]
        high = spectrum.astype(jnp.bfloat16)
        low = (spectrum - high.astype(jnp.float32)).astype(jnp.bfloat16)
        left = jnp.dot(high, table_ref[...], preferred_element_type=jnp.float32)
        right = jnp.dot(low, table_ref[:, :LAGS], preferred_element_type=jnp.float32)
        lagged = left[:, :LAGS] + (left[:, LAGS:] + right)
        member = jnp.bitwise_xor(owner, mine) * wins + win
        out_ref[member] = lagged if out_ref.dtype == jnp.float32 else encode(lagged)
        return 0

    lax.fori_loop(0, near * wins, part_of, 0)


def per_device(records, block_pairs, lag_low, lag_high, slot_count):
    segments, channels, length = records.shape
    blocks = channels // BLOCK
    chans, wins = lax.axis_size("chan"), lax.axis_size("win")
    both = ("chan", "win")
    near = REACH // blocks
    parts, chips, halves = near * wins, near // 2 * wins, near // 2
    width = BLOCK // parts
    rows = blocks * segments * width
    slots = block_pairs.shape[0]
    share = slots // wins
    group_total = chans // near
    group, member = lax.axis_index("chan") // near, lax.axis_index("chan") % near

    def partner(block, distance):
        return lax.ppermute(block, both, [(i, i ^ distance) for i in range(chans * wins)])

    def along(block, to):
        route = [(q * near + j, to(q) * near + j) for q in range(group_total) for j in range(near)]
        return lax.ppermute(block, "chan", [r for r in route if 0 <= r[1] < chans])

    split = whitened_parts(records, block_pairs, slot_count, near, wins)
    split = split.reshape(halves, 2, wins, rows + NOTE_ROWS, 2 * F)
    other = partner(split[:, 1], wins)
    keep = split[:, 0]

    planes, notes = [[], [], []], []
    for w in range(wins):
        for h in range(halves):
            piece = [keep[h, w, :rows], other[h, w, :rows]]
            if w == 0:
                piece += [keep[h, w, rows:], other[h, w, rows:]]
            piece = jnp.concatenate(piece, axis=0)
            if w or h:
                piece = partner(piece, h * 2 * wins + w)
            if w == 0:
                notes.append(piece[2 * rows :].reshape(2, NOTE_ROWS, 2 * F)[:, :3, :slots])
            sent = piece[: 2 * rows]
            planes[0].append(along(sent, lambda q: q ^ 1))
            planes[1].append(piece)
            planes[2].append(along(sent, lambda q: ((q + 1) ^ 1) - 1))

    notes = jnp.concatenate(notes, axis=0).astype(jnp.int32)
    level, rest = notes[:, :2] // REACH, notes[:, :2] % REACH
    level = jnp.where(group % 2 == 0, 2 - level, level)
    place = jnp.bitwise_xor(rest // blocks, member) * blocks + rest % blocks
    place = (level * (wins * REACH) + place) * (segments * width)
    firsts, seconds = place[:, 0].reshape(near * slots), place[:, 1].reshape(near * slots)
    counts = notes[:, 2, 0]

    fold = max(width, 16)
    scale = 2.0 ** math.floor(31 - 0.5 * math.log2(F * segments * wins))
    table = inverse_tables(length, scale / math.sqrt(F * segments * wins))
    hbm = pl.BlockSpec(memory_space=pl.ANY)
    smem = pl.BlockSpec(memory_space=pltpu.SMEM)
    vmem = pl.BlockSpec(memory_space=pltpu.VMEM)
    lagged = pl.pallas_call(
        functools.partial(pair_kernel, near, wins, fold),
        in_specs=[smem, smem, smem, vmem] + [hbm] * (3 * chips),
        out_specs=vmem,
        out_shape=jax.ShapeDtypeStruct(
            (parts, share * fold, LAGS), jnp.bfloat16 if fold == width else jnp.float32
        ),
        scratch_shapes=[
            pltpu.VMEM((3 * chips * 2 * rows, 2 * F), jnp.bfloat16),
            pltpu.VMEM((share * fold, 2 * F), jnp.float32),
            pltpu.SemaphoreType.DMA((3 * chips,)),
        ],
        compiler_params=pltpu.CompilerParams(vmem_limit_bytes=VMEM_LIMIT),
    )(firsts, seconds, counts, table, *planes[0], *planes[1], *planes[2])
    if fold > width:
        lagged = encode(lagged.reshape(parts, share, fold // width, width, LAGS).sum(axis=2))
        lagged = lagged.reshape(parts, share * width, LAGS)

    groups = [[q * parts + k for k in range(parts)] for q in range(group_total)]
    stack = lax.all_to_all(lagged, both, 0, 0, axis_index_groups=groups, tiled=True)
    stack = decode(stack.reshape(parts, share, width, LAGS), 1.0 / scale)
    stack = stack.transpose(1, 0, 2, 3).reshape(share, BLOCK, LAGS)
    start = lax.axis_index("win") * share
    low = lax.dynamic_slice_in_dim(lag_low, start, share)
    high = lax.dynamic_slice_in_dim(lag_high, start, share)
    lag_index = jnp.arange(LAGS, dtype=jnp.int32)[None, :]
    used = start + jnp.arange(share, dtype=jnp.int32) < slot_count[0]
    keep = (lag_index >= low[:, None]) & (lag_index < high[:, None]) & used[:, None]
    return jnp.where(keep[:, None, :], stack, jnp.zeros_like(stack))


def solution(mesh):
    in_specs = (P("win", "chan", None), P("chan", None), P("chan"), P("chan"), P("chan"))
    out_specs = P(("chan", "win"), None, None)
    return jax.shard_map(
        per_device, mesh=mesh, in_specs=in_specs, out_specs=out_specs, check_vma=False
    )
```

```python
import functools
import math

import jax
import jax.numpy as jnp
import numpy as np
from jax import lax
from jax.experimental import pallas as pl
from jax.experimental.pallas import tpu as pltpu
from jax.sharding import PartitionSpec as P

BLOCK = 128
F = 128
LAGS = 128
REACH = 16
NOTE_ROWS = 16
VMEM_LIMIT = 48 * 1024 * 1024
SPECTRA_VMEM = VMEM_LIMIT


def forward_table(length):
    first = length // 32
    times = np.arange(length, dtype=np.int64)[:, None]
    freqs = (first + np.arange(F, dtype=np.int64))[None, :]
    phase = 2.0 * math.pi / length * (times * freqs % length)
    table = np.concatenate([np.cos(phase), -np.sin(phase)], axis=1)
    return jnp.asarray(table.astype(np.float32)).astype(jnp.bfloat16)


def inverse_tables(length, factor):
    first = length // 32
    freqs = (first + np.arange(F, dtype=np.int64))[:, None]
    shifts = (np.arange(LAGS, dtype=np.int64) - LAGS // 2)[None, :]
    phase = 2.0 * math.pi / length * (freqs * shifts % length)
    table = (np.concatenate([np.cos(phase), -np.sin(phase)], axis=0) * factor).astype(np.float32)
    high = table.astype(jnp.bfloat16)
    low = (table - high.astype(np.float32)).astype(jnp.bfloat16)
    return jnp.asarray(np.concatenate([high, low], axis=1))


def encode(values):
    values = values * jnp.abs(values)
    return (values * jnp.abs(values)).astype(jnp.bfloat16)


def spectra_kernel(near, wins, records, pairs, count_ref, table, out_ref, held, pairs_held, table_held, note, sem):
    segments, channels, _ = records.shape
    cut, blocks = out_ref.shape[0], channels // BLOCK
    width = BLOCK // cut
    chan = lax.axis_index("chan")
    mine = lax.rem(chan, near) * wins + lax.axis_index("win")
    copies = [
        pltpu.make_async_copy(records.at[s], held.at[s], sem.at[s]) for s in range(segments)
    ]
    table_copy = pltpu.make_async_copy(table, table_held, sem.at[segments])
    pairs_copy = pltpu.make_async_copy(pairs, pairs_held, sem.at[segments + 1])
    table_copy.start()
    for copy in copies:
        copy.start()
    pairs_copy.start()
    table_copy.wait()
    for s in range(segments):
        copies[s].wait()
        for block in range(blocks):
            rows = held[s, pl.ds(block * BLOCK, BLOCK), :]
            spectra = jnp.dot(rows, table_held[...], preferred_element_type=jnp.float32)
            real_part, imag_part = spectra[:, :F], spectra[:, F:]
            power = real_part * real_part + imag_part * imag_part
            level = jnp.mean(power, axis=-1, keepdims=True)
            scale = lax.rsqrt(power + 0.1 * level + 1e-06)
            whitened = jnp.concatenate([real_part * scale, imag_part * scale], axis=1)
            whitened = whitened.astype(jnp.bfloat16)
            spot = pl.ds((block * segments + s) * width, width)
            if cut == 1:
                out_ref[0, spot, :] = whitened
            else:
                for part in range(cut):
                    piece = whitened[part * width : (part + 1) * width]
                    out_ref[jnp.bitwise_xor(mine, part), spot, :] = piece
    pairs_copy.wait()
    base = (lax.div(chan, near) - 1) * REACH
    slots = pairs.shape[1]
    note[...] = jnp.zeros_like(note)
    note[0:2, 0:slots] = jnp.clip(pairs_held[...] - base, 0, 3 * REACH - 1).astype(jnp.float32)
    note[2:3, :] = jnp.full((1, note.shape[1]), count_ref[0], jnp.int32).astype(jnp.float32)
    notes = note[...].astype(jnp.bfloat16)
    for part in range(cut):
        out_ref[part, pl.ds(out_ref.shape[1] - NOTE_ROWS, NOTE_ROWS), :] = notes


def whitened_parts(records, block_pairs, slot_count, near, wins):
    segments, channels, length = records.shape
    blocks, parts = channels // BLOCK, near * wins
    width = BLOCK // parts
    packed = width % 16 == 0
    cut = parts if packed else 1
    rows = blocks * segments * BLOCK // cut
    hbm = pl.BlockSpec(memory_space=pl.ANY)
    vmem = pl.BlockSpec(memory_space=pltpu.VMEM)
    smem = pl.BlockSpec(memory_space=pltpu.SMEM)
    out = pl.pallas_call(
        functools.partial(spectra_kernel, near, wins),
        in_specs=[hbm, hbm, smem, hbm],
        out_specs=vmem,
        out_shape=jax.ShapeDtypeStruct((cut, rows + NOTE_ROWS, 2 * F), jnp.bfloat16),
        scratch_shapes=[
            pltpu.VMEM(records.shape, jnp.bfloat16),
            pltpu.VMEM(block_pairs.shape[::-1], jnp.int32),
            pltpu.VMEM((length, 2 * F), jnp.bfloat16),
            pltpu.VMEM((NOTE_ROWS, 2 * F), jnp.float32),
            pltpu.SemaphoreType.DMA((segments + 2,)),
        ],
        compiler_params=pltpu.CompilerParams(vmem_limit_bytes=SPECTRA_VMEM),
    )(records, block_pairs.T, slot_count, forward_table(length))
    if packed:
        return out
    mine = lax.axis_index("chan") % near * wins + lax.axis_index("win")
    split = out[0, :rows].reshape(blocks, segments, parts, width, 2 * F)
    split = split.transpose(2, 0, 1, 3, 4).reshape(parts, blocks * segments * width, 2 * F)
    split = jnp.take(split, jnp.bitwise_xor(mine, jnp.arange(parts)), axis=0)
    notes = jnp.broadcast_to(out[0, rows:], (parts, NOTE_ROWS, 2 * F))
    return jnp.concatenate([split, notes], axis=1)


def gather_pieces(pieces, held, sem):
    size = held.shape[0] // len(pieces)
    copies = [
        pltpu.make_async_copy(
            piece.at[pl.ds(0, size)], held.at[pl.ds(k * size, size)], sem.at[k]
        )
        for k, piece in enumerate(pieces)
    ]
    for copy in copies:
        copy.start()
    for copy in copies:
        copy.wait()


def add_pairs(near, wins, windows, fold, firsts, seconds, counts, held, before, cross):
    plane = held.shape[0] // (3 * windows)
    rows = plane // REACH
    slots = cross.shape[0] // (near * wins * fold)
    together = min(4, slots)

    def one_pair(index):
        first, second = firsts[index], seconds[index]
        spot = pl.ds(pl.multiple_of(index * fold, fold), fold)
        if before is None:
            real_sum = jnp.zeros((fold, F), jnp.float32)
            imag_sum = jnp.zeros((fold, F), jnp.float32)
        else:
            real_sum = before[spot, pl.ds(0, F)]
            imag_sum = before[spot, pl.ds(F, F)]
        for w in range(windows):
            for r in range(0, rows, 16):
                a = held[pl.ds(pl.multiple_of(first + (w * plane + r), 16), 16), :]
                b = held[pl.ds(pl.multiple_of(second + (w * plane + r), 16), 16), :]
                a, b = a.astype(jnp.float32), b.astype(jnp.float32)
                ar, ai, br, bi = a[:, :F], a[:, F:], b[:, :F], b[:, F:]
                real_sum += ar * br + ai * bi
                imag_sum += ar * bi - ai * br
        cross[spot, pl.ds(0, F)] = real_sum
        cross[spot, pl.ds(F, F)] = imag_sum

    def owner_of(owner, _):
        def some_pairs(step, _):
            for k in range(together):
                one_pair(owner * (slots * wins) + step * together + k)
            return 0

        count = jnp.clip(counts[owner], 0, slots * wins)
        lax.fori_loop(0, lax.div(count + (together - 1), together), some_pairs, 0)
        return 0

    lax.fori_loop(0, near, owner_of, 0)


def first_kernel(near, wins, fold, firsts, seconds, counts, *refs):
    pieces, (cross, held, sem) = refs[:-3], refs[-3:]
    gather_pieces(pieces, held, sem)
    add_pairs(near, wins, 1, fold, firsts, seconds, counts, held, None, cross)


def last_kernel(near, wins, fold, firsts, seconds, counts, before, table_ref, *refs):
    pieces, (out_ref, held, cross, sem) = refs[:-4], refs[-4:]
    gather_pieces(pieces, held, sem)
    add_pairs(near, wins, wins - 1, fold, firsts, seconds, counts, held, before, cross)
    mine = lax.rem(lax.axis_index("chan"), near)
    span = cross.shape[0] // near
    for owner in range(near):
        spectrum = cross[pl.ds(owner * span, span), :]
        high = spectrum.astype(jnp.bfloat16)
        low = (spectrum - high.astype(jnp.float32)).astype(jnp.bfloat16)
        left = jnp.dot(high, table_ref[...], preferred_element_type=jnp.float32)
        right = jnp.dot(low, table_ref[:, :LAGS], preferred_element_type=jnp.float32)
        lagged = left[:, :LAGS] + (left[:, LAGS:] + right)
        lagged = lagged if out_ref.dtype == jnp.float32 else encode(lagged)
        out_ref[jnp.bitwise_xor(owner, mine)] = lagged


def stack_kernel(share, scale, code, low_ref, high_ref, count_ref, out, held, sem):
    parts, width = code.shape[0], code.shape[1] // share
    start = lax.axis_index("win") * share
    lag_index = lax.broadcasted_iota(jnp.int32, (parts, width, LAGS), 2)
    together = min(4, share)
    copies = []
    for slot in range(share):
        values = code[:, pl.ds(slot * width, width), :].astype(jnp.float32)
        root = lax.rsqrt(lax.rsqrt(jnp.abs(values))) * scale
        root = jnp.where(values < 0, -root, root)
        used = start + slot < count_ref[0]
        high = jnp.where(used, high_ref[start + slot], 0)
        keep = (lag_index >= low_ref[start + slot]) & (lag_index < high)
        held[slot] = jnp.where(keep, root, 0.0).reshape(BLOCK, LAGS)
        if slot % together == together - 1:
            spot = pl.ds(slot + 1 - together, together)
            copies.append(pltpu.make_async_copy(held.at[spot], out.at[spot], sem.at[len(copies)]))
            copies[-1].start()
    for copy in copies:
        copy.wait()


def per_device(records, block_pairs, lag_low, lag_high, slot_count):
    segments, channels, length = records.shape
    blocks = channels // BLOCK
    chans, wins = lax.axis_size("chan"), lax.axis_size("win")
    both = ("chan", "win")
    near = REACH // blocks
    parts, chips, halves = near * wins, near // 2 * wins, near // 2
    width = BLOCK // parts
    rows = blocks * segments * width
    slots = block_pairs.shape[0]
    share = slots // wins
    group_total = chans // near
    group, member = lax.axis_index("chan") // near, lax.axis_index("chan") % near

    def partner(block, distance):
        return lax.ppermute(block, both, [(i, i ^ distance) for i in range(chans * wins)])

    def along(block, to):
        route = [(q * near + j, to(q) * near + j) for q in range(group_total) for j in range(near)]
        return lax.ppermute(block, "chan", [r for r in route if 0 <= r[1] < chans])

    split = whitened_parts(records, block_pairs, slot_count, near, wins)
    split = split.reshape(halves, 2, wins, rows + NOTE_ROWS, 2 * F)
    other = partner(split[:, 1], wins)
    keep = split[:, 0]

    planes, notes = [[], [], []], []
    for w in range(wins):
        for h in range(halves):
            piece = [keep[h, w, :rows], other[h, w, :rows]]
            if w == 0:
                piece += [keep[h, w, rows:], other[h, w, rows:]]
            piece = jnp.concatenate(piece, axis=0)
            if len(planes[1]) >= 3:
                piece = lax.optimization_barrier((piece, planes[1][-2]))[0]
            if w or h:
                piece = partner(piece, h * 2 * wins + w)
            if w == 0:
                notes.append(piece[2 * rows :].reshape(2, NOTE_ROWS, 2 * F)[:, :3, :slots])
            sent = piece[: 2 * rows]
            if len(planes[0]) >= 2:
                sent = lax.optimization_barrier((sent, planes[0][-2], planes[2][-2]))[0]
            planes[0].append(along(sent, lambda q: q ^ 1))
            planes[1].append(piece)
            planes[2].append(along(sent, lambda q: ((q + 1) ^ 1) - 1))

    notes = jnp.concatenate(notes, axis=0).astype(jnp.int32)
    level, rest = notes[:, :2] // REACH, notes[:, :2] % REACH
    level = jnp.where(group % 2 == 0, 2 - level, level)
    place = jnp.bitwise_xor(rest // blocks, member) * blocks + rest % blocks
    def first_row(windows):
        row = (level * (windows * REACH) + place) * (segments * width)
        return row[:, 0].reshape(near * slots), row[:, 1].reshape(near * slots), counts

    counts = notes[:, 2, 0]
    fold = max(width, 16)
    scale = 2.0 ** math.floor(31 - 0.5 * math.log2(F * segments * wins))
    table = inverse_tables(length, scale / math.sqrt(F * segments * wins))
    hbm = pl.BlockSpec(memory_space=pl.ANY)
    smem = pl.BlockSpec(memory_space=pltpu.SMEM)
    vmem = pl.BlockSpec(memory_space=pltpu.VMEM)
    params = pltpu.CompilerParams(vmem_limit_bytes=VMEM_LIMIT)
    cross = jax.ShapeDtypeStruct((near * slots * fold, 2 * F), jnp.float32)
    first = [plane[:halves] for plane in planes]
    first = first[0] + first[1] + first[2]
    before = pl.pallas_call(
        functools.partial(first_kernel, near, wins, fold),
        in_specs=[smem, smem, smem] + [hbm] * len(first),
        out_specs=vmem,
        out_shape=cross,
        scratch_shapes=[
            pltpu.VMEM((len(first) * 2 * rows, 2 * F), jnp.bfloat16),
            pltpu.SemaphoreType.DMA((len(first),)),
        ],
        compiler_params=params,
    )(*first_row(1), *first)
    last = [plane[halves:] for plane in planes]
    last = last[0] + last[1] + last[2]
    lagged = pl.pallas_call(
        functools.partial(last_kernel, near, wins, fold),
        in_specs=[smem, smem, smem, vmem, vmem] + [hbm] * len(last),
        out_specs=vmem,
        out_shape=jax.ShapeDtypeStruct(
            (near, slots * fold, LAGS), jnp.bfloat16 if fold == width else jnp.float32
        ),
        scratch_shapes=[
            pltpu.VMEM((len(last) * 2 * rows, 2 * F), jnp.bfloat16),
            pltpu.VMEM(cross.shape, jnp.float32),
            pltpu.SemaphoreType.DMA((len(last),)),
        ],
        compiler_params=params,
    )(*first_row(wins - 1), before, table, *last)
    if fold > width:
        lagged = encode(lagged.reshape(near, slots, fold // width, width, LAGS).sum(axis=2))
    lagged = lagged.reshape(parts, share * width, LAGS)

    groups = [[q * parts + k for k in range(parts)] for q in range(group_total)]
    stack = lax.all_to_all(lagged, both, 0, 0, axis_index_groups=groups, tiled=True)
    return pl.pallas_call(
        functools.partial(stack_kernel, share, 1.0 / scale),
        in_specs=[vmem, smem, smem, smem],
        out_specs=hbm,
        out_shape=jax.ShapeDtypeStruct((share, BLOCK, LAGS), jnp.float32),
        scratch_shapes=[
            pltpu.VMEM((share, BLOCK, LAGS), jnp.float32),
            pltpu.SemaphoreType.DMA((max(1, share // 4),)),
        ],
        compiler_params=params,
    )(stack, lag_low, lag_high, slot_count)


def solution(mesh):
    in_specs = (P("win", "chan", None), P("chan", None), P("chan"), P("chan"), P("chan"))
    out_specs = P(("chan", "win"), None, None)
    return jax.shard_map(
        per_device, mesh=mesh, in_specs=in_specs, out_specs=out_specs, check_vma=False
    )
```

```python
import functools
import math

import jax
import jax.numpy as jnp
import numpy as np
from jax import lax
from jax.experimental import pallas as pl
from jax.experimental.pallas import tpu as pltpu
from jax.sharding import PartitionSpec as P

BLOCK = 128
F = 128
LAGS = 128
REACH = 16
NOTE_ROWS = 16
VMEM_LIMIT = 48 * 1024 * 1024
SPECTRA_VMEM = 52 * 1024 * 1024


def fill_forward_table(table_ref):
    length = table_ref.shape[0]
    first = length // 32
    step = 64
    for start in range(0, length, step):
        times = start + lax.broadcasted_iota(jnp.int32, (step, F), 0)
        freqs = first + lax.broadcasted_iota(jnp.int32, (step, F), 1)
        turns = lax.rem(times * freqs, length).astype(jnp.float32) * (1.0 / length)
        half = jnp.minimum(turns, 1.0 - turns)
        angle = 2.0 * math.pi * jnp.minimum(half, 0.5 - half)
        square = angle * angle
        sine, cosine = 1.0, 1.0
        for k in range(6, 0, -1):
            sine = 1.0 - square * sine * (1.0 / (2 * k * (2 * k + 1)))
        for k in range(7, 0, -1):
            cosine = 1.0 - square * cosine * (1.0 / (2 * k * (2 * k - 1)))
        sine = sine * angle
        sine = jnp.where(turns < 0.5, -sine, sine)
        cosine = jnp.where(half <= 0.25, cosine, -cosine)
        table_ref[pl.ds(start, step), pl.ds(0, F)] = cosine.astype(jnp.bfloat16)
        table_ref[pl.ds(start, step), pl.ds(F, F)] = sine.astype(jnp.bfloat16)


def inverse_tables(length, factor):
    first = length // 32
    freqs = (first + np.arange(F, dtype=np.int64))[:, None]
    shifts = (np.arange(LAGS, dtype=np.int64) - LAGS // 2)[None, :]
    phase = 2.0 * math.pi / length * (freqs * shifts % length)
    table = (np.concatenate([np.cos(phase), -np.sin(phase)], axis=0) * factor).astype(np.float32)
    high = table.astype(jnp.bfloat16)
    low = (table - high.astype(np.float32)).astype(jnp.bfloat16)
    return jnp.asarray(np.concatenate([high, low], axis=1))


def encode(values):
    values = values * jnp.abs(values)
    return (values * jnp.abs(values)).astype(jnp.bfloat16)


def spectra_kernel(near, wins, records, out_ref, held, table, sem):
    segments, channels, _ = records.shape
    cut, blocks = out_ref.shape[0], channels // BLOCK
    width = BLOCK // cut
    mine = lax.rem(lax.axis_index("chan"), near) * wins + lax.axis_index("win")
    copies = [
        pltpu.make_async_copy(records.at[s], held.at[s], sem.at[s]) for s in range(segments)
    ]
    for copy in copies:
        copy.start()
    fill_forward_table(table)

    def whitened(s, block):
        rows = held[s, pl.ds(block * BLOCK, BLOCK), :]
        spectra = jnp.dot(rows, table[...], preferred_element_type=jnp.float32)
        real_part, imag_part = spectra[:, :F], spectra[:, F:]
        power = real_part * real_part + imag_part * imag_part
        level = jnp.mean(power, axis=-1, keepdims=True)
        scale = lax.rsqrt(power + 0.1 * level + 1e-06)
        return jnp.concatenate([real_part * scale, imag_part * scale], axis=1)

    together = max(1, 16 // width)
    for s in range(0, segments, together):
        for k in range(together):
            copies[s + k].wait()
        for block in range(blocks):
            values = [whitened(s + k, block) for k in range(together)]
            for part in range(cut):
                tile = [v[part * width : (part + 1) * width] for v in values]
                tile = jnp.concatenate(tile, axis=0) if together > 1 else tile[0]
                spot = pl.ds((block * segments + s) * width, together * width)
                number = jnp.bitwise_xor(mine, part) if cut > 1 else 0
                out_ref[number, spot, :] = tile.astype(jnp.bfloat16)


def whitened_parts(records, near, wins):
    segments, channels, length = records.shape
    blocks, parts = channels // BLOCK, near * wins
    width = BLOCK // parts
    packed = width % 8 == 0
    cut = parts if packed else 1
    rows = blocks * segments * BLOCK // cut
    hbm = pl.BlockSpec(memory_space=pl.ANY)
    out = pl.pallas_call(
        functools.partial(spectra_kernel, near, wins),
        in_specs=[hbm],
        out_specs=pl.BlockSpec(memory_space=pltpu.VMEM),
        out_shape=jax.ShapeDtypeStruct((cut, rows, 2 * F), jnp.bfloat16),
        scratch_shapes=[
            pltpu.VMEM(records.shape, jnp.bfloat16),
            pltpu.VMEM((length, 2 * F), jnp.bfloat16),
            pltpu.SemaphoreType.DMA((segments,)),
        ],
        compiler_params=pltpu.CompilerParams(vmem_limit_bytes=SPECTRA_VMEM),
    )(records)
    if packed:
        return out
    mine = lax.axis_index("chan") % near * wins + lax.axis_index("win")
    split = out.reshape(blocks, segments, parts, width, 2 * F)
    split = split.transpose(2, 0, 1, 3, 4).reshape(parts, rows // parts, 2 * F)
    return jnp.take(split, jnp.bitwise_xor(mine, jnp.arange(parts)), axis=0)


def gather(moves, held, sem):
    copies, spot = [], 0
    for k, (ref, first, count) in enumerate(moves):
        copies.append(
            pltpu.make_async_copy(
                ref.at[pl.ds(first, count)], held.at[pl.ds(spot, count)], sem.at[k]
            )
        )
        spot += count
        copies[-1].start()
    for copy in copies:
        copy.wait()


def add_pairs(near, fold, slots_ref, held, tiles, before, cross):
    slots = (slots_ref.shape[0] - near - 1) // (2 * near + 2)
    together = min(4, slots)

    def one_pair(index):
        first, second = slots_ref[index], slots_ref[near * slots + index]
        spot = pl.ds(pl.multiple_of(index * fold, fold), fold)
        real_sum, imag_sum = None, None
        for tile in tiles:
            a = held[pl.ds(pl.multiple_of(first + tile, 16), 16), :].astype(jnp.float32)
            b = held[pl.ds(pl.multiple_of(second + tile, 16), 16), :].astype(jnp.float32)
            ar, ai, br, bi = a[:, :F], a[:, F:], b[:, :F], b[:, F:]
            real_part, imag_part = ar * br + ai * bi, ar * bi - ai * br
            real_sum = real_part if real_sum is None else real_sum + real_part
            imag_sum = imag_part if imag_sum is None else imag_sum + imag_part
        if fold == 8:
            real_sum = real_sum[:8] + real_sum[8:]
            imag_sum = imag_sum[:8] + imag_sum[8:]
        if before is not None:
            real_sum += before[spot, pl.ds(0, F)]
            imag_sum += before[spot, pl.ds(F, F)]
        cross[spot, pl.ds(0, F)] = real_sum
        cross[spot, pl.ds(F, F)] = imag_sum

    def owner_of(owner, _):
        def some_pairs(step, _):
            for k in range(together):
                one_pair(owner * slots + step * together + k)
            return 0

        count = jnp.clip(slots_ref[2 * near * slots + owner], 0, slots)
        lax.fori_loop(0, lax.div(count + (together - 1), together), some_pairs, 0)
        return 0

    lax.fori_loop(0, near, owner_of, 0)


def first_kernel(near, fold, size, rows, slots_ref, *refs):
    pieces, (cross, held, sem) = refs[:6], refs[6:]
    part = (near - 2) * size
    moves = []
    for plane in range(3):
        moves += [(pieces[plane], 0, 2 * size), (pieces[3 + plane], 0, part)]
    gather(moves, held, sem)
    add_pairs(near, fold, slots_ref, held, list(range(0, rows, 16)), None, cross)


def last_kernel(near, fold, windows, size, rows, slots_ref, before, table, *refs):
    pieces, (out_ref, held, cross, table_ref, sem) = refs[:6], refs[6:]
    table_copy = pltpu.make_async_copy(table, table_ref, sem.at[6])
    table_copy.start()
    part = (near - 2) * size
    moves = []
    for plane in range(3):
        piece, last = pieces[plane], pieces[3 + plane]
        moves += [(piece, part, piece.shape[0] - part), (last, 0, 2 * size)]
    gather(moves, held, sem)
    tiles = [w * near * size + r for w in range(windows) for r in range(0, rows, 16)]
    add_pairs(near, fold, slots_ref, held, tiles, before, cross)
    table_copy.wait()
    mine = lax.rem(lax.axis_index("chan"), near)
    span = cross.shape[0] // near
    for owner in range(near):
        spectrum = cross[pl.ds(owner * span, span), :]
        high = spectrum.astype(jnp.bfloat16)
        low = (spectrum - high.astype(jnp.float32)).astype(jnp.bfloat16)
        left = jnp.dot(high, table_ref[...], preferred_element_type=jnp.float32)
        right = jnp.dot(low, table_ref[:, :LAGS], preferred_element_type=jnp.float32)
        lagged = left[:, :LAGS] + (left[:, LAGS:] + right)
        lagged = lagged if out_ref.dtype == jnp.float32 else encode(lagged)
        out_ref[jnp.bitwise_xor(owner, mine)] = lagged


def stack_kernel(near, width, scale, slots_ref, *refs):
    codes, (out, held, sem) = refs[:-3], refs[-3:]
    share, parts = held.shape[0], codes[0].shape[0]
    slots = (slots_ref.shape[0] - near - 1) // (2 * near + 2)
    limits = 2 * near * slots + near
    start = lax.axis_index("win") * share
    lag_index = lax.broadcasted_iota(jnp.int32, (parts, width, LAGS), 2)
    together = min(4, share)
    copies = []
    for slot in range(share):
        tile = slot * width // 16 * 16
        at = limits + start + slot
        high = jnp.where(start + slot < slots_ref[limits + 2 * slots], slots_ref[at + slots], 0)
        keep = (lag_index >= slots_ref[at]) & (lag_index < high)
        kept = []
        for code in codes:
            values = code[:, pl.ds(tile, 16), :].astype(jnp.float32)
            values = values[:, slot * width - tile : slot * width - tile + width, :]
            root = lax.rsqrt(lax.rsqrt(jnp.abs(values))) * scale
            root = jnp.where(values < 0, -root, root)
            kept.append(jnp.where(keep, root, 0.0))
        kept = jnp.concatenate(kept, axis=1) if len(kept) > 1 else kept[0]
        held[slot] = kept.reshape(BLOCK, LAGS)
        if slot % together == together - 1:
            spot = pl.ds(slot + 1 - together, together)
            copies.append(pltpu.make_async_copy(held.at[spot], out.at[spot], sem.at[len(copies)]))
            copies[-1].start()
    for copy in copies:
        copy.wait()


def per_device(records, block_pairs, lag_low, lag_high, slot_count):
    segments, channels, length = records.shape
    blocks = channels // BLOCK
    chans, wins = lax.axis_size("chan"), lax.axis_size("win")
    both = ("chan", "win")
    near = REACH // blocks
    parts, halves = near * wins, near // 2
    width = BLOCK // parts
    rows = segments * width
    size = blocks * rows
    slots = block_pairs.shape[0]
    share = slots // wins
    group_total = chans // near
    group, member = lax.axis_index("chan") // near, lax.axis_index("chan") % near

    def partner(block, distance):
        return lax.ppermute(block, both, [(i, i ^ distance) for i in range(chans * wins)])

    def along(block, to):
        route = [(q * near + j, to(q) * near + j) for q in range(group_total) for j in range(near)]
        return lax.ppermute(block, "chan", [r for r in route if 0 <= r[1] < chans])

    def even(block):
        return along(block, lambda q: q ^ 1)

    def odd(block):
        return along(block, lambda q: ((q + 1) ^ 1) - 1)

    def after(block, *others):
        return lax.optimization_barrier((block,) + others)[0]

    near_blocks = jnp.clip(block_pairs.T - (group - 1) * REACH, 0, 3 * REACH - 1)
    note = jnp.pad(near_blocks, ((0, NOTE_ROWS - 2), (0, 2 * F - slots)))
    note = jnp.where(jnp.arange(NOTE_ROWS)[:, None] == 2, slot_count[0], note).astype(jnp.bfloat16)

    split = whitened_parts(records, near, wins)
    split = split.reshape(halves, 2, wins, size, 2 * F)
    sent = split[:, 1].reshape(halves * wins * size, 2 * F)
    other = partner(jnp.concatenate([sent, note], axis=0), wins)
    other_note = other[halves * wins * size :]
    other = other[: halves * wins * size].reshape(halves, wins, size, 2 * F)

    order = [(w, h) for w in range(wins) for h in range(halves)]
    own, notes = [], []
    for w, h in order:
        piece = [split[h, 0, w], other[h, w]] + ([note, other_note] if w == 0 else [])
        piece = jnp.concatenate(piece, axis=0)
        if (w, h) == order[-1]:
            piece = after(piece, own[2])
        if w or h:
            piece = partner(piece, h * 2 * wins + w)
        if w == 0:
            notes.append(piece[2 * size :].reshape(2, NOTE_ROWS, 2 * F)[:, :3, :slots])
        own.append(piece[: 2 * size])
    rounds = [own[0], jnp.concatenate(own[1:-1], axis=0), own[-1]]
    planes = []
    for k, sent in enumerate(rounds):
        sent = after(sent, planes[0][0], planes[0][2]) if k == 2 else sent
        planes.append([even(sent), sent, odd(sent)])

    notes = jnp.concatenate(notes, axis=0).astype(jnp.int32)
    level, rest = notes[:, :2] // REACH, notes[:, :2] % REACH
    level = jnp.where(group % 2 == 0, 2 - level, level)
    member_block = (jnp.bitwise_xor(rest // blocks, member), rest % blocks)
    counts = notes[:, 2, 0]

    def first_row(windows):
        row = (level * (windows * near) + member_block[0]) * size + member_block[1] * rows
        row = [row[:, 0].reshape(near * slots), row[:, 1].reshape(near * slots)]
        return jnp.concatenate(row + [counts, lag_low, lag_high, slot_count])

    fold = 16 if width % 16 == 0 else 8
    scale = 2.0 ** math.floor(31 - 0.5 * math.log2(F * segments * wins))
    table = inverse_tables(length, scale / math.sqrt(F * segments * wins))
    hbm = pl.BlockSpec(memory_space=pl.ANY)
    smem = pl.BlockSpec(memory_space=pltpu.SMEM)
    vmem = pl.BlockSpec(memory_space=pltpu.VMEM)
    params = pltpu.CompilerParams(vmem_limit_bytes=VMEM_LIMIT)
    cross = jax.ShapeDtypeStruct((near * slots * fold, 2 * F), jnp.float32)
    table_rows, last_rows = first_row(1), first_row(wins - 1)
    before = pl.pallas_call(
        functools.partial(first_kernel, near, fold, size, rows),
        in_specs=[smem] + [hbm] * 6,
        out_specs=vmem,
        out_shape=cross,
        scratch_shapes=[
            pltpu.VMEM((3 * near * size, 2 * F), jnp.bfloat16),
            pltpu.SemaphoreType.DMA((6,)),
        ],
        compiler_params=params,
    )(table_rows, *planes[0], *planes[1])

    groups = [[q * parts + k for k in range(parts)] for q in range(group_total)]
    lagged = pl.pallas_call(
        functools.partial(last_kernel, near, fold, wins - 1, size, rows),
        in_specs=[smem, vmem, hbm] + [hbm] * 6,
        out_specs=vmem,
        out_shape=jax.ShapeDtypeStruct(
            (near, slots * fold, LAGS), jnp.bfloat16 if fold == width else jnp.float32
        ),
        scratch_shapes=[
            pltpu.VMEM((3 * (wins - 1) * near * size, 2 * F), jnp.bfloat16),
            pltpu.VMEM(cross.shape, jnp.float32),
            pltpu.VMEM(table.shape, table.dtype),
            pltpu.SemaphoreType.DMA((7,)),
        ],
        compiler_params=params,
    )(last_rows, before, table, *planes[1], *planes[2])
    if fold > width:
        lagged = encode(lagged.reshape(near, slots, fold // width, width, LAGS).sum(axis=2))
    lagged = lagged.reshape(parts, share * width, LAGS)
    code = lax.all_to_all(lagged, both, 0, 0, axis_index_groups=groups, tiled=True)

    return pl.pallas_call(
        functools.partial(stack_kernel, near, width, 1.0 / scale),
        in_specs=[smem, vmem],
        out_specs=hbm,
        out_shape=jax.ShapeDtypeStruct((share, BLOCK, LAGS), jnp.float32),
        scratch_shapes=[
            pltpu.VMEM((share, BLOCK, LAGS), jnp.float32),
            pltpu.SemaphoreType.DMA((max(1, share // 4),)),
        ],
        compiler_params=params,
    )(table_rows, code)


def solution(mesh):
    in_specs = (P("win", "chan", None), P("chan", None), P("chan"), P("chan"), P("chan"))
    out_specs = P(("chan", "win"), None, None)
    return jax.shard_map(
        per_device, mesh=mesh, in_specs=in_specs, out_specs=out_specs, check_vma=False
    )
```

```python
import functools
import math

import jax
import jax.numpy as jnp
import numpy as np
from jax import lax
from jax.experimental import pallas as pl
from jax.experimental.pallas import tpu as pltpu
from jax.sharding import PartitionSpec as P

BLOCK = 128
F = 128
LAGS = 128
REACH = 16
NOTE_ROWS = 16
VMEM_LIMIT = 48 * 1024 * 1024
SPECTRA_VMEM = 52 * 1024 * 1024


def fill_forward_table(table_ref):
    length = table_ref.shape[0]
    first = length // 32
    step = 64
    for start in range(0, length, step):
        times = start + lax.broadcasted_iota(jnp.int32, (step, F), 0)
        freqs = first + lax.broadcasted_iota(jnp.int32, (step, F), 1)
        turns = lax.rem(times * freqs, length).astype(jnp.float32) * (1.0 / length)
        half = jnp.minimum(turns, 1.0 - turns)
        angle = 2.0 * math.pi * jnp.minimum(half, 0.5 - half)
        square = angle * angle
        sine, cosine = 1.0, 1.0
        for k in range(6, 0, -1):
            sine = 1.0 - square * sine * (1.0 / (2 * k * (2 * k + 1)))
        for k in range(7, 0, -1):
            cosine = 1.0 - square * cosine * (1.0 / (2 * k * (2 * k - 1)))
        sine = sine * angle
        sine = jnp.where(turns < 0.5, -sine, sine)
        cosine = jnp.where(half <= 0.25, cosine, -cosine)
        table_ref[pl.ds(start, step), pl.ds(0, F)] = cosine.astype(jnp.bfloat16)
        table_ref[pl.ds(start, step), pl.ds(F, F)] = sine.astype(jnp.bfloat16)


def inverse_tables(length, factor):
    first = length // 32
    freqs = (first + np.arange(F, dtype=np.int64))[:, None]
    shifts = (np.arange(LAGS, dtype=np.int64) - LAGS // 2)[None, :]
    phase = 2.0 * math.pi / length * (freqs * shifts % length)
    table = (np.concatenate([np.cos(phase), -np.sin(phase)], axis=0) * factor).astype(np.float32)
    high = table.astype(jnp.bfloat16)
    low = (table - high.astype(np.float32)).astype(jnp.bfloat16)
    return jnp.asarray(np.concatenate([high, low], axis=1))


def encode(values):
    values = values * jnp.abs(values)
    return (values * jnp.abs(values)).astype(jnp.bfloat16)


def spectra_kernel(near, wins, records, out_ref, held, table, sem):
    segments, channels, _ = records.shape
    cut, blocks = out_ref.shape[0], channels // BLOCK
    width = BLOCK // cut
    mine = lax.rem(lax.axis_index("chan"), near) * wins + lax.axis_index("win")
    copies = [
        pltpu.make_async_copy(records.at[s], held.at[s], sem.at[s]) for s in range(segments)
    ]
    for copy in copies:
        copy.start()
    fill_forward_table(table)

    def whitened(s, block):
        rows = held[s, pl.ds(block * BLOCK, BLOCK), :]
        spectra = jnp.dot(rows, table[...], preferred_element_type=jnp.float32)
        real_part, imag_part = spectra[:, :F], spectra[:, F:]
        power = real_part * real_part + imag_part * imag_part
        level = jnp.mean(power, axis=-1, keepdims=True)
        scale = lax.rsqrt(power + 0.1 * level + 1e-06)
        return jnp.concatenate([real_part * scale, imag_part * scale], axis=1)

    together = max(2, 16 // width)
    for s in range(0, segments, together):
        for k in range(together):
            copies[s + k].wait()
        for block in range(blocks):
            values = [whitened(s + k, block) for k in range(together)]
            for part in range(cut):
                tile = [v[part * width : (part + 1) * width] for v in values]
                tile = jnp.concatenate(tile, axis=0) if together > 1 else tile[0]
                spot = pl.ds((block * segments + s) * width, together * width)
                number = jnp.bitwise_xor(mine, part) if cut > 1 else 0
                out_ref[number, spot, :] = tile.astype(jnp.bfloat16)


def whitened_parts(records, near, wins):
    segments, channels, length = records.shape
    blocks, parts = channels // BLOCK, near * wins
    width = BLOCK // parts
    packed = width % 8 == 0
    cut = parts if packed else 1
    rows = blocks * segments * BLOCK // cut
    hbm = pl.BlockSpec(memory_space=pl.ANY)
    out = pl.pallas_call(
        functools.partial(spectra_kernel, near, wins),
        in_specs=[hbm],
        out_specs=pl.BlockSpec(memory_space=pltpu.VMEM),
        out_shape=jax.ShapeDtypeStruct((cut, rows, 2 * F), jnp.bfloat16),
        scratch_shapes=[
            pltpu.VMEM(records.shape, jnp.bfloat16),
            pltpu.VMEM((length, 2 * F), jnp.bfloat16),
            pltpu.SemaphoreType.DMA((segments,)),
        ],
        compiler_params=pltpu.CompilerParams(vmem_limit_bytes=SPECTRA_VMEM),
    )(records)
    if packed:
        return out
    mine = lax.axis_index("chan") % near * wins + lax.axis_index("win")
    split = out.reshape(blocks, segments, parts, width, 2 * F)
    split = split.transpose(2, 0, 1, 3, 4).reshape(parts, rows // parts, 2 * F)
    return jnp.take(split, jnp.bitwise_xor(mine, jnp.arange(parts)), axis=0)


def gather(moves, held, sem, others=()):
    copies, spot = [], 0
    for k, (ref, first, count) in enumerate(moves):
        copies.append(
            pltpu.make_async_copy(
                ref.at[pl.ds(first, count)], held.at[pl.ds(spot, count)], sem.at[k]
            )
        )
        spot += count
        copies[-1].start()
    for copy in others:
        copy.start()
    for copy in copies:
        copy.wait()


def add_pairs(near, fold, slots_ref, held, tiles, cross, copies):
    slots = (slots_ref.shape[0] - near - 1) // (2 * near + 2)
    together = min(4, slots)

    def one_pair(index):
        first, second = slots_ref[index], slots_ref[near * slots + index]
        spot = pl.ds(pl.multiple_of(index * fold, fold), fold)
        real_sum, imag_sum = None, None
        for tile in tiles:
            a = held[pl.ds(pl.multiple_of(first + tile, 16), 16), :].astype(jnp.float32)
            b = held[pl.ds(pl.multiple_of(second + tile, 16), 16), :].astype(jnp.float32)
            ar, ai, br, bi = a[:, :F], a[:, F:], b[:, :F], b[:, F:]
            real_part, imag_part = ar * br + ai * bi, ar * bi - ai * br
            real_sum = real_part if real_sum is None else real_sum + real_part
            imag_sum = imag_part if imag_sum is None else imag_sum + imag_part
        if fold == 8:
            real_sum = real_sum[:8] + real_sum[8:]
            imag_sum = imag_sum[:8] + imag_sum[8:]
        if copies:
            real_sum += cross[spot, pl.ds(0, F)]
            imag_sum += cross[spot, pl.ds(F, F)]
        cross[spot, pl.ds(0, F)] = real_sum
        cross[spot, pl.ds(F, F)] = imag_sum

    for owner in range(near):
        if copies:
            copies[owner].wait()

        def some_pairs(step, _):
            for k in range(together):
                one_pair(owner * slots + step * together + k)
            return 0

        count = jnp.clip(slots_ref[2 * near * slots + owner], 0, slots)
        lax.fori_loop(0, lax.div(count + (together - 1), together), some_pairs, 0)


def first_kernel(near, fold, size, rows, slots_ref, *refs):
    pieces, (cross, held, sem) = refs[:6], refs[6:]
    part = (near - 2) * size
    moves = []
    for plane in range(3):
        moves += [(pieces[plane], 0, 2 * size), (pieces[3 + plane], 0, part)]
    gather(moves, held, sem)
    add_pairs(near, fold, slots_ref, held, list(range(0, rows, 16)), cross, [])


def last_kernel(near, fold, windows, size, rows, slots_ref, before, table, *refs):
    pieces, (out_ref, held, cross, table_ref, sem) = refs[:6], refs[6:]
    table_copy = pltpu.make_async_copy(table, table_ref, sem.at[6])
    table_copy.start()
    span = cross.shape[0] // near
    copies = []
    for owner in range(near):
        spot = pl.ds(owner * span, span)
        copies.append(pltpu.make_async_copy(before.at[spot], cross.at[spot], sem.at[7 + owner]))
    part = (near - 2) * size
    moves = []
    for plane in range(3):
        piece, last = pieces[plane], pieces[3 + plane]
        moves += [(piece, part, piece.shape[0] - part), (last, 0, 2 * size)]
    gather(moves, held, sem, copies)
    tiles = [w * near * size + r for w in range(windows) for r in range(0, rows, 16)]
    add_pairs(near, fold, slots_ref, held, tiles, cross, copies)
    table_copy.wait()
    mine = lax.rem(lax.axis_index("chan"), near)
    for owner in range(near):
        spectrum = cross[pl.ds(owner * span, span), :]
        high = spectrum.astype(jnp.bfloat16)
        low = (spectrum - high.astype(jnp.float32)).astype(jnp.bfloat16)
        left = jnp.dot(high, table_ref[...], preferred_element_type=jnp.float32)
        right = jnp.dot(low, table_ref[:, :LAGS], preferred_element_type=jnp.float32)
        lagged = left[:, :LAGS] + (left[:, LAGS:] + right)
        lagged = lagged if out_ref.dtype == jnp.float32 else encode(lagged)
        out_ref[jnp.bitwise_xor(owner, mine)] = lagged


def stack_kernel(near, width, scale, slots_ref, *refs):
    codes, (out, held, sem) = refs[:-3], refs[-3:]
    share, parts = held.shape[0], codes[0].shape[0]
    slots = (slots_ref.shape[0] - near - 1) // (2 * near + 2)
    limits = 2 * near * slots + near
    start = lax.axis_index("win") * share
    lag_index = lax.broadcasted_iota(jnp.int32, (parts, width, LAGS), 2)
    together = min(4, share)
    copies = []
    for slot in range(share):
        tile = slot * width // 16 * 16
        at = limits + start + slot
        high = jnp.where(start + slot < slots_ref[limits + 2 * slots], slots_ref[at + slots], 0)
        keep = (lag_index >= slots_ref[at]) & (lag_index < high)
        kept = []
        for code in codes:
            values = code[:, pl.ds(tile, 16), :].astype(jnp.float32)
            values = values[:, slot * width - tile : slot * width - tile + width, :]
            root = lax.rsqrt(lax.rsqrt(jnp.abs(values))) * scale
            root = jnp.where(values < 0, -root, root)
            kept.append(jnp.where(keep, root, 0.0))
        kept = jnp.concatenate(kept, axis=1) if len(kept) > 1 else kept[0]
        held[slot] = kept.reshape(BLOCK, LAGS)
        if slot % together == together - 1:
            spot = pl.ds(slot + 1 - together, together)
            copies.append(pltpu.make_async_copy(held.at[spot], out.at[spot], sem.at[len(copies)]))
            copies[-1].start()
    for copy in copies:
        copy.wait()


def per_device(records, block_pairs, lag_low, lag_high, slot_count):
    segments, channels, length = records.shape
    blocks = channels // BLOCK
    chans, wins = lax.axis_size("chan"), lax.axis_size("win")
    both = ("chan", "win")
    near = REACH // blocks
    parts, halves = near * wins, near // 2
    width = BLOCK // parts
    rows = segments * width
    size = blocks * rows
    slots = block_pairs.shape[0]
    share = slots // wins
    group_total = chans // near
    group, member = lax.axis_index("chan") // near, lax.axis_index("chan") % near

    def partner(block, distance):
        return lax.ppermute(block, both, [(i, i ^ distance) for i in range(chans * wins)])

    def along(block, to):
        route = [(q * near + j, to(q) * near + j) for q in range(group_total) for j in range(near)]
        return lax.ppermute(block, "chan", [r for r in route if 0 <= r[1] < chans])

    def even(block):
        return along(block, lambda q: q ^ 1)

    def odd(block):
        return along(block, lambda q: ((q + 1) ^ 1) - 1)

    def after(block, *others):
        return lax.optimization_barrier((block,) + others)[0]

    near_blocks = jnp.clip(block_pairs.T - (group - 1) * REACH, 0, 3 * REACH - 1)
    note = jnp.pad(near_blocks, ((0, NOTE_ROWS - 2), (0, 2 * F - slots)))
    note = jnp.where(jnp.arange(NOTE_ROWS)[:, None] == 2, slot_count[0], note).astype(jnp.bfloat16)

    split = whitened_parts(records, near, wins)
    split = split.reshape(halves, 2, wins, size, 2 * F)
    sent = split[:, 1].reshape(halves * wins * size, 2 * F)
    other = partner(jnp.concatenate([sent, note], axis=0), wins)
    other_note = other[halves * wins * size :]
    other = other[: halves * wins * size].reshape(halves, wins, size, 2 * F)

    order = [(w, h) for w in range(wins) for h in range(halves)]
    own, notes = [], []
    for w, h in order:
        piece = [split[h, 0, w], other[h, w]] + ([note, other_note] if w == 0 else [])
        piece = jnp.concatenate(piece, axis=0)
        if (w, h) == order[-1]:
            piece = after(piece, own[2])
        if w or h:
            piece = partner(piece, h * 2 * wins + w)
        if w == 0:
            notes.append(piece[2 * size :].reshape(2, NOTE_ROWS, 2 * F)[:, :3, :slots])
        own.append(piece[: 2 * size])
    rounds = [own[0], jnp.concatenate(own[1:-1], axis=0), own[-1]]
    planes = []
    for k, sent in enumerate(rounds):
        sent = after(sent, planes[0][0], planes[0][2]) if k == 2 else sent
        planes.append([even(sent), sent, odd(sent)])

    notes = jnp.concatenate(notes, axis=0).astype(jnp.int32)
    level, rest = notes[:, :2] // REACH, notes[:, :2] % REACH
    level = jnp.where(group % 2 == 0, 2 - level, level)
    member_block = (jnp.bitwise_xor(rest // blocks, member), rest % blocks)
    counts = notes[:, 2, 0]

    def first_row(windows):
        row = (level * (windows * near) + member_block[0]) * size + member_block[1] * rows
        row = [row[:, 0].reshape(near * slots), row[:, 1].reshape(near * slots)]
        return jnp.concatenate(row + [counts, lag_low, lag_high, slot_count])

    fold = 16 if width % 16 == 0 else 8
    scale = 2.0 ** math.floor(31 - 0.5 * math.log2(F * segments * wins))
    table = inverse_tables(length, scale / math.sqrt(F * segments * wins))
    hbm = pl.BlockSpec(memory_space=pl.ANY)
    smem = pl.BlockSpec(memory_space=pltpu.SMEM)
    vmem = pl.BlockSpec(memory_space=pltpu.VMEM)
    params = pltpu.CompilerParams(vmem_limit_bytes=VMEM_LIMIT)
    cross = jax.ShapeDtypeStruct((near * slots * fold, 2 * F), jnp.float32)
    table_rows, last_rows = first_row(1), first_row(wins - 1)
    before = pl.pallas_call(
        functools.partial(first_kernel, near, fold, size, rows),
        in_specs=[smem] + [hbm] * 6,
        out_specs=vmem,
        out_shape=cross,
        scratch_shapes=[
            pltpu.VMEM((3 * near * size, 2 * F), jnp.bfloat16),
            pltpu.SemaphoreType.DMA((6,)),
        ],
        compiler_params=params,
    )(table_rows, *planes[0], *planes[1])

    groups = [[q * parts + k for k in range(parts)] for q in range(group_total)]
    lagged = pl.pallas_call(
        functools.partial(last_kernel, near, fold, wins - 1, size, rows),
        in_specs=[smem, hbm, hbm] + [hbm] * 6,
        out_specs=vmem,
        out_shape=jax.ShapeDtypeStruct(
            (near, slots * fold, LAGS), jnp.bfloat16 if fold == width else jnp.float32
        ),
        scratch_shapes=[
            pltpu.VMEM((3 * (wins - 1) * near * size, 2 * F), jnp.bfloat16),
            pltpu.VMEM(cross.shape, jnp.float32),
            pltpu.VMEM(table.shape, table.dtype),
            pltpu.SemaphoreType.DMA((7 + near,)),
        ],
        compiler_params=params,
    )(last_rows, before, table, *planes[1], *planes[2])
    if fold > width:
        lagged = encode(lagged.reshape(near, slots, fold // width, width, LAGS).sum(axis=2))
    lagged = lagged.reshape(parts, share * width, LAGS)
    code = lax.all_to_all(lagged, both, 0, 0, axis_index_groups=groups, tiled=True)

    return pl.pallas_call(
        functools.partial(stack_kernel, near, width, 1.0 / scale),
        in_specs=[smem, vmem],
        out_specs=hbm,
        out_shape=jax.ShapeDtypeStruct((share, BLOCK, LAGS), jnp.float32),
        scratch_shapes=[
            pltpu.VMEM((share, BLOCK, LAGS), jnp.float32),
            pltpu.SemaphoreType.DMA((max(1, share // 4),)),
        ],
        compiler_params=params,
    )(table_rows, code)


def solution(mesh):
    in_specs = (P("win", "chan", None), P("chan", None), P("chan"), P("chan"), P("chan"))
    out_specs = P(("chan", "win"), None, None)
    return jax.shard_map(
        per_device, mesh=mesh, in_specs=in_specs, out_specs=out_specs, check_vma=False
    )
```

```python
import functools
import math

import jax
import jax.numpy as jnp
import numpy as np
from jax import lax
from jax.experimental import pallas as pl
from jax.experimental.pallas import tpu as pltpu
from jax.sharding import PartitionSpec as P

BLOCK = 128
F = 128
LAGS = 128
REACH = 16
NOTE_ROWS = 16
VMEM_LIMIT = 48 * 1024 * 1024
SPECTRA_VMEM = 52 * 1024 * 1024


def fill_forward_table(table_ref):
    length = table_ref.shape[0]
    first = length // 32
    step = 64
    for start in range(0, length, step):
        times = start + lax.broadcasted_iota(jnp.int32, (step, F), 0)
        freqs = first + lax.broadcasted_iota(jnp.int32, (step, F), 1)
        turns = lax.rem(times * freqs, length).astype(jnp.float32) * (1.0 / length)
        half = jnp.minimum(turns, 1.0 - turns)
        angle = 2.0 * math.pi * jnp.minimum(half, 0.5 - half)
        square = angle * angle
        sine, cosine = 1.0, 1.0
        for k in range(6, 0, -1):
            sine = 1.0 - square * sine * (1.0 / (2 * k * (2 * k + 1)))
        for k in range(7, 0, -1):
            cosine = 1.0 - square * cosine * (1.0 / (2 * k * (2 * k - 1)))
        sine = sine * angle
        sine = jnp.where(turns < 0.5, -sine, sine)
        cosine = jnp.where(half <= 0.25, cosine, -cosine)
        table_ref[pl.ds(start, step), pl.ds(0, F)] = cosine.astype(jnp.bfloat16)
        table_ref[pl.ds(start, step), pl.ds(F, F)] = sine.astype(jnp.bfloat16)


def inverse_tables(length, factor):
    first = length // 32
    freqs = (first + np.arange(F, dtype=np.int64))[:, None]
    shifts = (np.arange(LAGS, dtype=np.int64) - LAGS // 2)[None, :]
    phase = 2.0 * math.pi / length * (freqs * shifts % length)
    table = (np.concatenate([np.cos(phase), -np.sin(phase)], axis=0) * factor).astype(np.float32)
    high = table.astype(jnp.bfloat16)
    low = (table - high.astype(np.float32)).astype(jnp.bfloat16)
    return jnp.asarray(np.concatenate([high, low], axis=1))


def encode(values):
    values = values * jnp.abs(values)
    return (values * jnp.abs(values)).astype(jnp.bfloat16)


def spectra_kernel(near, wins, records, out_ref, held, table, sem):
    segments, channels, _ = records.shape
    cut, blocks = out_ref.shape[0], channels // BLOCK
    width = BLOCK // cut
    mine = lax.rem(lax.axis_index("chan"), near) * wins + lax.axis_index("win")
    copies = [
        pltpu.make_async_copy(records.at[s], held.at[s], sem.at[s]) for s in range(segments)
    ]
    for copy in copies:
        copy.start()
    fill_forward_table(table)

    def whitened(s, block):
        rows = held[s, pl.ds(block * BLOCK, BLOCK), :]
        spectra = jnp.dot(rows, table[...], preferred_element_type=jnp.float32)
        real_part, imag_part = spectra[:, :F], spectra[:, F:]
        power = real_part * real_part + imag_part * imag_part
        level = jnp.mean(power, axis=-1, keepdims=True)
        scale = lax.rsqrt(power + 0.1 * level + 1e-06)
        return jnp.concatenate([real_part * scale, imag_part * scale], axis=1)

    together = max(2, 16 // width)
    for s in range(0, segments, together):
        for k in range(together):
            copies[s + k].wait()
        for block in range(blocks):
            values = [whitened(s + k, block) for k in range(together)]
            for part in range(cut):
                tile = [v[part * width : (part + 1) * width] for v in values]
                tile = jnp.concatenate(tile, axis=0) if together > 1 else tile[0]
                spot = pl.ds((block * segments + s) * width, together * width)
                number = jnp.bitwise_xor(mine, part) if cut > 1 else 0
                out_ref[number, spot, :] = tile.astype(jnp.bfloat16)


def whitened_parts(records, near, wins):
    segments, channels, length = records.shape
    blocks, parts = channels // BLOCK, near * wins
    width = BLOCK // parts
    packed = width % 8 == 0
    cut = parts if packed else 1
    rows = blocks * segments * BLOCK // cut
    hbm = pl.BlockSpec(memory_space=pl.ANY)
    out = pl.pallas_call(
        functools.partial(spectra_kernel, near, wins),
        in_specs=[hbm],
        out_specs=pl.BlockSpec(memory_space=pltpu.VMEM),
        out_shape=jax.ShapeDtypeStruct((cut, rows, 2 * F), jnp.bfloat16),
        scratch_shapes=[
            pltpu.VMEM(records.shape, jnp.bfloat16),
            pltpu.VMEM((length, 2 * F), jnp.bfloat16),
            pltpu.SemaphoreType.DMA((segments,)),
        ],
        compiler_params=pltpu.CompilerParams(vmem_limit_bytes=SPECTRA_VMEM),
    )(records)
    if packed:
        return out
    mine = lax.axis_index("chan") % near * wins + lax.axis_index("win")
    split = out.reshape(blocks, segments, parts, width, 2 * F)
    split = split.transpose(2, 0, 1, 3, 4).reshape(parts, rows // parts, 2 * F)
    return jnp.take(split, jnp.bitwise_xor(mine, jnp.arange(parts)), axis=0)


def gather(moves, held, sem, others=()):
    copies, spot = [], 0
    for k, (ref, first, count) in enumerate(moves):
        copies.append(
            pltpu.make_async_copy(
                ref.at[pl.ds(first, count)], held.at[pl.ds(spot, count)], sem.at[k]
            )
        )
        spot += count
        copies[-1].start()
    for copy in others:
        copy.start()
    for copy in copies:
        copy.wait()


def add_pairs(near, fold, slots_ref, held, tiles, cross, copies):
    slots = (slots_ref.shape[0] - near - 1) // (2 * near + 2)
    together = min(4, slots)

    def one_pair(index):
        first, second = slots_ref[index], slots_ref[near * slots + index]
        spot = pl.ds(pl.multiple_of(index * fold, fold), fold)
        real_sum, imag_sum = None, None
        for tile in tiles:
            a = held[pl.ds(pl.multiple_of(first + tile, 16), 16), :].astype(jnp.float32)
            b = held[pl.ds(pl.multiple_of(second + tile, 16), 16), :].astype(jnp.float32)
            ar, ai, br, bi = a[:, :F], a[:, F:], b[:, :F], b[:, F:]
            real_part, imag_part = ar * br + ai * bi, ar * bi - ai * br
            real_sum = real_part if real_sum is None else real_sum + real_part
            imag_sum = imag_part if imag_sum is None else imag_sum + imag_part
        if fold == 8:
            real_sum = real_sum[:8] + real_sum[8:]
            imag_sum = imag_sum[:8] + imag_sum[8:]
        if copies:
            real_sum += cross[spot, pl.ds(0, F)]
            imag_sum += cross[spot, pl.ds(F, F)]
        cross[spot, pl.ds(0, F)] = real_sum
        cross[spot, pl.ds(F, F)] = imag_sum

    for owner in range(near):
        if copies:
            copies[owner].wait()

        def some_pairs(step, _):
            for k in range(together):
                one_pair(owner * slots + step * together + k)
            return 0

        count = jnp.clip(slots_ref[2 * near * slots + owner], 0, slots)
        lax.fori_loop(0, lax.div(count + (together - 1), together), some_pairs, 0)


def first_kernel(near, fold, size, rows, slots_ref, *refs):
    pieces, (cross, held, sem) = refs[:6], refs[6:]
    part = (near - 2) * size
    moves = []
    for plane in range(3):
        moves += [(pieces[plane], 0, 2 * size), (pieces[3 + plane], 0, part)]
    gather(moves, held, sem)
    add_pairs(near, fold, slots_ref, held, list(range(0, rows, 16)), cross, [])


def last_kernel(near, fold, windows, size, rows, slot_rows, before, table, *refs):
    pieces, (out_ref, held, cross, table_ref, slots_ref, sem) = refs[:6], refs[6:]
    slots_copy = pltpu.make_async_copy(slot_rows, slots_ref, sem.at[7 + near])
    slots_copy.start()
    table_copy = pltpu.make_async_copy(table, table_ref, sem.at[6])
    table_copy.start()
    span = cross.shape[0] // near
    copies = []
    for owner in range(near):
        spot = pl.ds(owner * span, span)
        copies.append(pltpu.make_async_copy(before.at[spot], cross.at[spot], sem.at[7 + owner]))
    part = (near - 2) * size
    moves = []
    for plane in range(3):
        piece, last = pieces[plane], pieces[3 + plane]
        moves += [(piece, part, piece.shape[0] - part), (last, 0, 2 * size)]
    gather(moves, held, sem, copies)
    slots_copy.wait()
    tiles = [w * near * size + r for w in range(windows) for r in range(0, rows, 16)]
    add_pairs(near, fold, slots_ref, held, tiles, cross, copies)
    table_copy.wait()
    mine = lax.rem(lax.axis_index("chan"), near)
    for owner in range(near):
        spectrum = cross[pl.ds(owner * span, span), :]
        high = spectrum.astype(jnp.bfloat16)
        low = (spectrum - high.astype(jnp.float32)).astype(jnp.bfloat16)
        left = jnp.dot(high, table_ref[...], preferred_element_type=jnp.float32)
        right = jnp.dot(low, table_ref[:, :LAGS], preferred_element_type=jnp.float32)
        lagged = left[:, :LAGS] + (left[:, LAGS:] + right)
        lagged = lagged if out_ref.dtype == jnp.float32 else encode(lagged)
        out_ref[jnp.bitwise_xor(owner, mine)] = lagged


def stack_kernel(near, width, scale, slots_ref, *refs):
    codes, (out, held, sem) = refs[:-3], refs[-3:]
    share, parts = held.shape[0], codes[0].shape[0]
    slots = (slots_ref.shape[0] - near - 1) // (2 * near + 2)
    limits = 2 * near * slots + near
    start = lax.axis_index("win") * share
    lag_index = lax.broadcasted_iota(jnp.int32, (parts, width, LAGS), 2)
    together = min(4, share)
    copies = []
    for slot in range(share):
        tile = slot * width // 16 * 16
        at = limits + start + slot
        high = jnp.where(start + slot < slots_ref[limits + 2 * slots], slots_ref[at + slots], 0)
        keep = (lag_index >= slots_ref[at]) & (lag_index < high)
        kept = []
        for code in codes:
            values = code[:, pl.ds(tile, 16), :].astype(jnp.float32)
            values = values[:, slot * width - tile : slot * width - tile + width, :]
            root = lax.rsqrt(lax.rsqrt(jnp.abs(values))) * scale
            root = jnp.where(values < 0, -root, root)
            kept.append(jnp.where(keep & (values != 0), root, 0.0))
        kept = jnp.concatenate(kept, axis=1) if len(kept) > 1 else kept[0]
        held[slot] = kept.reshape(BLOCK, LAGS)
        if slot % together == together - 1:
            spot = pl.ds(slot + 1 - together, together)
            copies.append(pltpu.make_async_copy(held.at[spot], out.at[spot], sem.at[len(copies)]))
            copies[-1].start()
    for copy in copies:
        copy.wait()


def per_device(records, block_pairs, lag_low, lag_high, slot_count):
    segments, channels, length = records.shape
    blocks = channels // BLOCK
    chans, wins = lax.axis_size("chan"), lax.axis_size("win")
    both = ("chan", "win")
    near = REACH // blocks
    parts, halves = near * wins, near // 2
    width = BLOCK // parts
    rows = segments * width
    size = blocks * rows
    slots = block_pairs.shape[0]
    share = slots // wins
    group_total = chans // near
    group, member = lax.axis_index("chan") // near, lax.axis_index("chan") % near

    def partner(block, distance):
        return lax.ppermute(block, both, [(i, i ^ distance) for i in range(chans * wins)])

    def along(block, to):
        route = [(q * near + j, to(q) * near + j) for q in range(group_total) for j in range(near)]
        return lax.ppermute(block, "chan", [r for r in route if 0 <= r[1] < chans])

    def even(block):
        return along(block, lambda q: q ^ 1)

    def odd(block):
        return along(block, lambda q: ((q + 1) ^ 1) - 1)

    def after(block, *others):
        return lax.optimization_barrier((block,) + others)[0]

    near_blocks = jnp.clip(block_pairs.T - (group - 1) * REACH, 0, 3 * REACH - 1)
    note = jnp.pad(near_blocks, ((0, NOTE_ROWS - 2), (0, 2 * F - slots)))
    note = jnp.where(jnp.arange(NOTE_ROWS)[:, None] == 2, slot_count[0], note).astype(jnp.bfloat16)

    split = whitened_parts(records, near, wins)
    split = split.reshape(halves, 2, wins, size, 2 * F)
    sent = split[:, 1].reshape(halves * wins * size, 2 * F)
    other = partner(jnp.concatenate([sent, note], axis=0), wins)
    other_note = other[halves * wins * size :]
    other = other[: halves * wins * size].reshape(halves, wins, size, 2 * F)

    order = [(w, h) for w in range(wins) for h in range(halves)]
    own, notes = [], []
    for w, h in order:
        piece = [split[h, 0, w], other[h, w]] + ([note, other_note] if w == 0 else [])
        piece = jnp.concatenate(piece, axis=0)
        if (w, h) == order[-1]:
            piece = after(piece, own[2])
        if w or h:
            piece = partner(piece, h * 2 * wins + w)
        if w == 0:
            notes.append(piece[2 * size :].reshape(2, NOTE_ROWS, 2 * F)[:, :3, :slots])
        own.append(piece[: 2 * size])
    rounds = [own[0], jnp.concatenate(own[1:-1], axis=0), own[-1]]
    planes = []
    for k, sent in enumerate(rounds):
        sent = after(sent, planes[0][0], planes[0][2]) if k == 2 else sent
        planes.append([even(sent), sent, odd(sent)])

    notes = jnp.concatenate(notes, axis=0).astype(jnp.int32)
    level, rest = notes[:, :2] // REACH, notes[:, :2] % REACH
    level = jnp.where(group % 2 == 0, 2 - level, level)
    member_block = (jnp.bitwise_xor(rest // blocks, member), rest % blocks)
    counts = notes[:, 2, 0]

    def first_row(windows):
        row = (level * (windows * near) + member_block[0]) * size + member_block[1] * rows
        row = [row[:, 0].reshape(near * slots), row[:, 1].reshape(near * slots)]
        return jnp.concatenate(row + [counts, lag_low, lag_high, slot_count])

    fold = 16 if width % 16 == 0 else 8
    scale = 2.0 ** math.floor(31 - 0.5 * math.log2(F * segments * wins))
    table = inverse_tables(length, scale / math.sqrt(F * segments * wins))
    hbm = pl.BlockSpec(memory_space=pl.ANY)
    smem = pl.BlockSpec(memory_space=pltpu.SMEM)
    vmem = pl.BlockSpec(memory_space=pltpu.VMEM)
    params = pltpu.CompilerParams(vmem_limit_bytes=VMEM_LIMIT)
    cross = jax.ShapeDtypeStruct((near * slots * fold, 2 * F), jnp.float32)
    table_rows, last_rows = first_row(1), first_row(wins - 1)
    before = pl.pallas_call(
        functools.partial(first_kernel, near, fold, size, rows),
        in_specs=[smem] + [hbm] * 6,
        out_specs=vmem,
        out_shape=cross,
        scratch_shapes=[
            pltpu.VMEM((3 * near * size, 2 * F), jnp.bfloat16),
            pltpu.SemaphoreType.DMA((6,)),
        ],
        compiler_params=params,
    )(table_rows, *planes[0], *planes[1])

    groups = [[q * parts + k for k in range(parts)] for q in range(group_total)]
    lagged = pl.pallas_call(
        functools.partial(last_kernel, near, fold, wins - 1, size, rows),
        in_specs=[hbm, hbm, hbm] + [hbm] * 6,
        out_specs=vmem,
        out_shape=jax.ShapeDtypeStruct(
            (near, slots * fold, LAGS), jnp.bfloat16 if fold == width else jnp.float32
        ),
        scratch_shapes=[
            pltpu.VMEM((3 * (wins - 1) * near * size, 2 * F), jnp.bfloat16),
            pltpu.VMEM(cross.shape, jnp.float32),
            pltpu.VMEM(table.shape, table.dtype),
            pltpu.SMEM(last_rows.shape, jnp.int32),
            pltpu.SemaphoreType.DMA((8 + near,)),
        ],
        compiler_params=params,
    )(last_rows, before, table, *planes[1], *planes[2])
    if fold > width:
        lagged = encode(lagged.reshape(near, slots, fold // width, width, LAGS).sum(axis=2))
    lagged = lagged.reshape(parts, share * width, LAGS)
    code = lax.all_to_all(lagged, both, 0, 0, axis_index_groups=groups, tiled=True)

    return pl.pallas_call(
        functools.partial(stack_kernel, near, width, 1.0 / scale),
        in_specs=[smem, vmem],
        out_specs=hbm,
        out_shape=jax.ShapeDtypeStruct((share, BLOCK, LAGS), jnp.float32),
        scratch_shapes=[
            pltpu.VMEM((share, BLOCK, LAGS), jnp.float32),
            pltpu.SemaphoreType.DMA((max(1, share // 4),)),
        ],
        compiler_params=params,
    )(table_rows, code)


def solution(mesh):
    in_specs = (P("win", "chan", None), P("chan", None), P("chan"), P("chan"), P("chan"))
    out_specs = P(("chan", "win"), None, None)
    return jax.shard_map(
        per_device, mesh=mesh, in_specs=in_specs, out_specs=out_specs, check_vma=False
    )
```

```python
import functools
import math

import jax
import jax.numpy as jnp
import numpy as np
from jax import lax
from jax.experimental import pallas as pl
from jax.experimental.pallas import tpu as pltpu
from jax.sharding import PartitionSpec as P

BLOCK = 128
F = 128
LAGS = 128
REACH = 16
NOTE_ROWS = 16
VMEM_LIMIT = 48 * 1024 * 1024
SPECTRA_VMEM = 52 * 1024 * 1024


def fill_forward_table(table_ref):
    length = table_ref.shape[0]
    first = length // 32
    step = 64
    for start in range(0, length, step):
        times = start + lax.broadcasted_iota(jnp.int32, (step, F), 0)
        freqs = first + lax.broadcasted_iota(jnp.int32, (step, F), 1)
        turns = lax.rem(times * freqs, length).astype(jnp.float32) * (1.0 / length)
        half = jnp.minimum(turns, 1.0 - turns)
        angle = 2.0 * math.pi * jnp.minimum(half, 0.5 - half)
        square = angle * angle
        sine, cosine = 1.0, 1.0
        for k in range(6, 0, -1):
            sine = 1.0 - square * sine * (1.0 / (2 * k * (2 * k + 1)))
        for k in range(7, 0, -1):
            cosine = 1.0 - square * cosine * (1.0 / (2 * k * (2 * k - 1)))
        sine = sine * angle
        sine = jnp.where(turns < 0.5, -sine, sine)
        cosine = jnp.where(half <= 0.25, cosine, -cosine)
        table_ref[pl.ds(start, step), pl.ds(0, F)] = cosine.astype(jnp.bfloat16)
        table_ref[pl.ds(start, step), pl.ds(F, F)] = sine.astype(jnp.bfloat16)


def inverse_tables(length, factor):
    first = length // 32
    freqs = (first + np.arange(F, dtype=np.int64))[:, None]
    shifts = (np.arange(LAGS, dtype=np.int64) - LAGS // 2)[None, :]
    phase = 2.0 * math.pi / length * (freqs * shifts % length)
    table = (np.concatenate([np.cos(phase), -np.sin(phase)], axis=0) * factor).astype(np.float32)
    high = table.astype(jnp.bfloat16)
    low = (table - high.astype(np.float32)).astype(jnp.bfloat16)
    return jnp.asarray(np.concatenate([high, low], axis=1))


def encode(values):
    values = values * jnp.abs(values)
    return (values * jnp.abs(values)).astype(jnp.bfloat16)


def spectra_kernel(near, wins, records, out_ref, held, table, sem):
    segments, channels, _ = records.shape
    cut, blocks = out_ref.shape[0], channels // BLOCK
    width = BLOCK // cut
    mine = lax.rem(lax.axis_index("chan"), near) * wins + lax.axis_index("win")
    copies = [
        pltpu.make_async_copy(records.at[s], held.at[s], sem.at[s]) for s in range(segments)
    ]
    for copy in copies:
        copy.start()
    fill_forward_table(table)

    def whitened(s, block):
        rows = held[s, pl.ds(block * BLOCK, BLOCK), :]
        spectra = jnp.dot(rows, table[...], preferred_element_type=jnp.float32)
        real_part, imag_part = spectra[:, :F], spectra[:, F:]
        power = real_part * real_part + imag_part * imag_part
        level = jnp.mean(power, axis=-1, keepdims=True)
        scale = lax.rsqrt(power + 0.1 * level + 1e-06)
        return jnp.concatenate([real_part * scale, imag_part * scale], axis=1)

    together = max(2, 16 // width)
    for s in range(0, segments, together):
        for k in range(together):
            copies[s + k].wait()
        for block in range(blocks):
            values = [whitened(s + k, block) for k in range(together)]
            for part in range(cut):
                tile = [v[part * width : (part + 1) * width] for v in values]
                tile = jnp.concatenate(tile, axis=0) if together > 1 else tile[0]
                spot = pl.ds((block * segments + s) * width, together * width)
                number = jnp.bitwise_xor(mine, part) if cut > 1 else 0
                out_ref[number, spot, :] = tile.astype(jnp.bfloat16)


def whitened_parts(records, near, wins):
    segments, channels, length = records.shape
    blocks, parts = channels // BLOCK, near * wins
    width = BLOCK // parts
    packed = width % 8 == 0
    cut = parts if packed else 1
    rows = blocks * segments * BLOCK // cut
    hbm = pl.BlockSpec(memory_space=pl.ANY)
    out = pl.pallas_call(
        functools.partial(spectra_kernel, near, wins),
        in_specs=[hbm],
        out_specs=pl.BlockSpec(memory_space=pltpu.VMEM),
        out_shape=jax.ShapeDtypeStruct((cut, rows, 2 * F), jnp.bfloat16),
        scratch_shapes=[
            pltpu.VMEM(records.shape, jnp.bfloat16),
            pltpu.VMEM((length, 2 * F), jnp.bfloat16),
            pltpu.SemaphoreType.DMA((segments,)),
        ],
        compiler_params=pltpu.CompilerParams(vmem_limit_bytes=SPECTRA_VMEM),
    )(records)
    if packed:
        return out
    mine = lax.axis_index("chan") % near * wins + lax.axis_index("win")
    split = out.reshape(blocks, segments, parts, width, 2 * F)
    split = split.transpose(2, 0, 1, 3, 4).reshape(parts, rows // parts, 2 * F)
    return jnp.take(split, jnp.bitwise_xor(mine, jnp.arange(parts)), axis=0)


def gather(moves, held, sem, others=()):
    copies, spot = [], 0
    for k, (ref, first, count) in enumerate(moves):
        copies.append(
            pltpu.make_async_copy(
                ref.at[pl.ds(first, count)], held.at[pl.ds(spot, count)], sem.at[k]
            )
        )
        spot += count
        copies[-1].start()
    for copy in others:
        copy.start()
    for copy in copies:
        copy.wait()


def add_pairs(near, fold, slots_ref, held, tiles, cross, copies):
    slots = (slots_ref.shape[0] - near - 1) // (2 * near + 2)
    together = min(8, slots)

    def one_pair(index):
        first, second = slots_ref[index], slots_ref[near * slots + index]
        spot = pl.ds(pl.multiple_of(index * fold, fold), fold)
        real_sum, imag_sum = None, None
        for tile in tiles:
            a = held[pl.ds(pl.multiple_of(first + tile, 16), 16), :].astype(jnp.float32)
            b = held[pl.ds(pl.multiple_of(second + tile, 16), 16), :].astype(jnp.float32)
            ar, ai, br, bi = a[:, :F], a[:, F:], b[:, :F], b[:, F:]
            real_part, imag_part = ar * br + ai * bi, ar * bi - ai * br
            real_sum = real_part if real_sum is None else real_sum + real_part
            imag_sum = imag_part if imag_sum is None else imag_sum + imag_part
        if fold == 8:
            real_sum = real_sum[:8] + real_sum[8:]
            imag_sum = imag_sum[:8] + imag_sum[8:]
        if copies:
            real_sum += cross[spot, pl.ds(0, F)]
            imag_sum += cross[spot, pl.ds(F, F)]
        cross[spot, pl.ds(0, F)] = real_sum
        cross[spot, pl.ds(F, F)] = imag_sum

    for owner in range(near):
        if copies:
            copies[owner].wait()

        def some_pairs(step, _):
            for k in range(together):
                one_pair(owner * slots + step * together + k)
            return 0

        count = jnp.clip(slots_ref[2 * near * slots + owner], 0, slots)
        lax.fori_loop(0, lax.div(count + (together - 1), together), some_pairs, 0)


def first_kernel(near, fold, size, rows, slots_ref, *refs):
    pieces, (cross, held, sem) = refs[:6], refs[6:]
    part = (near - 2) * size
    moves = []
    for plane in range(3):
        moves += [(pieces[plane], 0, 2 * size), (pieces[3 + plane], 0, part)]
    gather(moves, held, sem)
    add_pairs(near, fold, slots_ref, held, list(range(0, rows, 16)), cross, [])


def last_kernel(near, fold, windows, size, rows, slot_rows, before, table, *refs):
    pieces, (out_ref, held, cross, table_ref, slots_ref, sem) = refs[:6], refs[6:]
    slots_copy = pltpu.make_async_copy(slot_rows, slots_ref, sem.at[7 + near])
    slots_copy.start()
    table_copy = pltpu.make_async_copy(table, table_ref, sem.at[6])
    table_copy.start()
    span = cross.shape[0] // near
    copies = []
    for owner in range(near):
        spot = pl.ds(owner * span, span)
        copies.append(pltpu.make_async_copy(before.at[spot], cross.at[spot], sem.at[7 + owner]))
    part = (near - 2) * size
    moves = []
    for plane in range(3):
        piece, last = pieces[plane], pieces[3 + plane]
        moves += [(piece, part, piece.shape[0] - part), (last, 0, 2 * size)]
    gather(moves, held, sem, copies)
    slots_copy.wait()
    tiles = [w * near * size + r for w in range(windows) for r in range(0, rows, 16)]
    add_pairs(near, fold, slots_ref, held, tiles, cross, copies)
    table_copy.wait()
    mine = lax.rem(lax.axis_index("chan"), near)
    for owner in range(near):
        spectrum = cross[pl.ds(owner * span, span), :]
        high = spectrum.astype(jnp.bfloat16)
        low = (spectrum - high.astype(jnp.float32)).astype(jnp.bfloat16)
        left = jnp.dot(high, table_ref[...], preferred_element_type=jnp.float32)
        right = jnp.dot(low, table_ref[:, :LAGS], preferred_element_type=jnp.float32)
        lagged = left[:, :LAGS] + (left[:, LAGS:] + right)
        lagged = lagged if out_ref.dtype == jnp.float32 else encode(lagged)
        out_ref[jnp.bitwise_xor(owner, mine)] = lagged


def stack_kernel(near, width, scale, slots_ref, *refs):
    codes, (out, held, sem) = refs[:-3], refs[-3:]
    share, parts = held.shape[0], codes[0].shape[0]
    slots = (slots_ref.shape[0] - near - 1) // (2 * near + 2)
    limits = 2 * near * slots + near
    start = lax.axis_index("win") * share
    lag_index = lax.broadcasted_iota(jnp.int32, (parts, width, LAGS), 2)
    together = min(4, share)
    copies = []
    for slot in range(share):
        tile = slot * width // 16 * 16
        at = limits + start + slot
        high = jnp.where(start + slot < slots_ref[limits + 2 * slots], slots_ref[at + slots], 0)
        keep = (lag_index >= slots_ref[at]) & (lag_index < high)
        kept = []
        for code in codes:
            values = code[:, pl.ds(tile, 16), :].astype(jnp.float32)
            values = values[:, slot * width - tile : slot * width - tile + width, :]
            root = lax.rsqrt(lax.rsqrt(jnp.abs(values))) * scale
            root = jnp.where(values < 0, -root, root)
            kept.append(jnp.where(keep & (values != 0), root, 0.0))
        kept = jnp.concatenate(kept, axis=1) if len(kept) > 1 else kept[0]
        held[slot] = kept.reshape(BLOCK, LAGS)
        if slot % together == together - 1:
            spot = pl.ds(slot + 1 - together, together)
            copies.append(pltpu.make_async_copy(held.at[spot], out.at[spot], sem.at[len(copies)]))
            copies[-1].start()
    for copy in copies:
        copy.wait()


def per_device(records, block_pairs, lag_low, lag_high, slot_count):
    segments, channels, length = records.shape
    blocks = channels // BLOCK
    chans, wins = lax.axis_size("chan"), lax.axis_size("win")
    both = ("chan", "win")
    near = REACH // blocks
    parts, halves = near * wins, near // 2
    width = BLOCK // parts
    rows = segments * width
    size = blocks * rows
    slots = block_pairs.shape[0]
    share = slots // wins
    group_total = chans // near
    group, member = lax.axis_index("chan") // near, lax.axis_index("chan") % near

    def partner(block, distance):
        return lax.ppermute(block, both, [(i, i ^ distance) for i in range(chans * wins)])

    def along(block, to):
        route = [(q * near + j, to(q) * near + j) for q in range(group_total) for j in range(near)]
        return lax.ppermute(block, "chan", [r for r in route if 0 <= r[1] < chans])

    def even(block):
        return along(block, lambda q: q ^ 1)

    def odd(block):
        return along(block, lambda q: ((q + 1) ^ 1) - 1)

    def after(block, *others):
        return lax.optimization_barrier((block,) + others)[0]

    near_blocks = jnp.clip(block_pairs.T - (group - 1) * REACH, 0, 3 * REACH - 1)
    note = jnp.pad(near_blocks, ((0, NOTE_ROWS - 2), (0, 2 * F - slots)))
    note = jnp.where(jnp.arange(NOTE_ROWS)[:, None] == 2, slot_count[0], note).astype(jnp.bfloat16)

    split = whitened_parts(records, near, wins)
    split = split.reshape(halves, 2, wins, size, 2 * F)
    sent = split[:, 1].reshape(halves * wins * size, 2 * F)
    other = partner(jnp.concatenate([sent, note], axis=0), wins)
    other_note = other[halves * wins * size :]
    other = other[: halves * wins * size].reshape(halves, wins, size, 2 * F)

    order = [(w, h) for w in range(wins) for h in range(halves)]
    own, notes = [], []
    for w, h in order:
        piece = [split[h, 0, w], other[h, w]] + ([note, other_note] if w == 0 else [])
        piece = jnp.concatenate(piece, axis=0)
        if (w, h) == order[-1]:
            piece = after(piece, own[2])
        if w or h:
            piece = partner(piece, h * 2 * wins + w)
        if w == 0:
            notes.append(piece[2 * size :].reshape(2, NOTE_ROWS, 2 * F)[:, :3, :slots])
        own.append(piece[: 2 * size])
    rounds = [own[0], jnp.concatenate(own[1:-1], axis=0), own[-1]]
    planes = []
    for k, sent in enumerate(rounds):
        sent = after(sent, planes[0][0], planes[0][2]) if k == 2 else sent
        planes.append([even(sent), sent, odd(sent)])

    notes = jnp.concatenate(notes, axis=0).astype(jnp.int32)
    level, rest = notes[:, :2] // REACH, notes[:, :2] % REACH
    level = jnp.where(group % 2 == 0, 2 - level, level)
    member_block = (jnp.bitwise_xor(rest // blocks, member), rest % blocks)
    counts = notes[:, 2, 0]

    def first_row(windows):
        row = (level * (windows * near) + member_block[0]) * size + member_block[1] * rows
        row = [row[:, 0].reshape(near * slots), row[:, 1].reshape(near * slots)]
        return jnp.concatenate(row + [counts, lag_low, lag_high, slot_count])

    fold = 16 if width % 16 == 0 else 8
    scale = 2.0 ** math.floor(31 - 0.5 * math.log2(F * segments * wins))
    table = inverse_tables(length, scale / math.sqrt(F * segments * wins))
    hbm = pl.BlockSpec(memory_space=pl.ANY)
    smem = pl.BlockSpec(memory_space=pltpu.SMEM)
    vmem = pl.BlockSpec(memory_space=pltpu.VMEM)
    params = pltpu.CompilerParams(vmem_limit_bytes=VMEM_LIMIT)
    cross = jax.ShapeDtypeStruct((near * slots * fold, 2 * F), jnp.float32)
    table_rows, last_rows = first_row(1), first_row(wins - 1)
    before = pl.pallas_call(
        functools.partial(first_kernel, near, fold, size, rows),
        in_specs=[smem] + [hbm] * 6,
        out_specs=vmem,
        out_shape=cross,
        scratch_shapes=[
            pltpu.VMEM((3 * near * size, 2 * F), jnp.bfloat16),
            pltpu.SemaphoreType.DMA((6,)),
        ],
        compiler_params=params,
    )(table_rows, *planes[0], *planes[1])

    groups = [[q * parts + k for k in range(parts)] for q in range(group_total)]
    lagged = pl.pallas_call(
        functools.partial(last_kernel, near, fold, wins - 1, size, rows),
        in_specs=[hbm, hbm, hbm] + [hbm] * 6,
        out_specs=vmem,
        out_shape=jax.ShapeDtypeStruct(
            (near, slots * fold, LAGS), jnp.bfloat16 if fold == width else jnp.float32
        ),
        scratch_shapes=[
            pltpu.VMEM((3 * (wins - 1) * near * size, 2 * F), jnp.bfloat16),
            pltpu.VMEM(cross.shape, jnp.float32),
            pltpu.VMEM(table.shape, table.dtype),
            pltpu.SMEM(last_rows.shape, jnp.int32),
            pltpu.SemaphoreType.DMA((8 + near,)),
        ],
        compiler_params=params,
    )(last_rows, before, table, *planes[1], *planes[2])
    if fold > width:
        lagged = encode(lagged.reshape(near, slots, fold // width, width, LAGS).sum(axis=2))
    lagged = lagged.reshape(parts, share * width, LAGS)
    code = lax.all_to_all(lagged, both, 0, 0, axis_index_groups=groups, tiled=True)

    return pl.pallas_call(
        functools.partial(stack_kernel, near, width, 1.0 / scale),
        in_specs=[smem, vmem],
        out_specs=hbm,
        out_shape=jax.ShapeDtypeStruct((share, BLOCK, LAGS), jnp.float32),
        scratch_shapes=[
            pltpu.VMEM((share, BLOCK, LAGS), jnp.float32),
            pltpu.SemaphoreType.DMA((max(1, share // 4),)),
        ],
        compiler_params=params,
    )(table_rows, code)


def solution(mesh):
    in_specs = (P("win", "chan", None), P("chan", None), P("chan"), P("chan"), P("chan"))
    out_specs = P(("chan", "win"), None, None)
    return jax.shard_map(
        per_device, mesh=mesh, in_specs=in_specs, out_specs=out_specs, check_vma=False
    )
```

```python
import functools
import math

import jax
import jax.numpy as jnp
import numpy as np
from jax import lax
from jax.experimental import pallas as pl
from jax.experimental.pallas import tpu as pltpu
from jax.sharding import PartitionSpec as P

BLOCK = 128
F = 128
LAGS = 128
REACH = 16
NOTE_ROWS = 16
VMEM_LIMIT = 48 * 1024 * 1024
SPECTRA_VMEM = 52 * 1024 * 1024


def fill_forward_table(table_ref):
    length = table_ref.shape[0]
    first = length // 32
    step = 64
    for start in range(0, length, step):
        times = start + lax.broadcasted_iota(jnp.int32, (step, F), 0)
        freqs = first + lax.broadcasted_iota(jnp.int32, (step, F), 1)
        turns = lax.rem(times * freqs, length).astype(jnp.float32) * (1.0 / length)
        half = jnp.minimum(turns, 1.0 - turns)
        angle = 2.0 * math.pi * jnp.minimum(half, 0.5 - half)
        square = angle * angle
        sine, cosine = 1.0, 1.0
        for k in range(6, 0, -1):
            sine = 1.0 - square * sine * (1.0 / (2 * k * (2 * k + 1)))
        for k in range(7, 0, -1):
            cosine = 1.0 - square * cosine * (1.0 / (2 * k * (2 * k - 1)))
        sine = sine * angle
        sine = jnp.where(turns < 0.5, -sine, sine)
        cosine = jnp.where(half <= 0.25, cosine, -cosine)
        table_ref[pl.ds(start, step), pl.ds(0, F)] = cosine.astype(jnp.bfloat16)
        table_ref[pl.ds(start, step), pl.ds(F, F)] = sine.astype(jnp.bfloat16)


def inverse_tables(length, factor):
    first = length // 32
    freqs = (first + np.arange(F, dtype=np.int64))[:, None]
    shifts = (np.arange(LAGS, dtype=np.int64) - LAGS // 2)[None, :]
    phase = 2.0 * math.pi / length * (freqs * shifts % length)
    table = (np.concatenate([np.cos(phase), -np.sin(phase)], axis=0) * factor).astype(np.float32)
    high = table.astype(jnp.bfloat16)
    low = (table - high.astype(np.float32)).astype(jnp.bfloat16)
    return jnp.asarray(np.concatenate([high, low], axis=1))


def encode(values):
    values = values * jnp.abs(values)
    return (values * jnp.abs(values)).astype(jnp.bfloat16)


def spectra_kernel(near, wins, records, out_ref, held, table, sem):
    segments, channels, _ = records.shape
    cut, blocks = out_ref.shape[0], channels // BLOCK
    width = BLOCK // cut
    mine = lax.rem(lax.axis_index("chan"), near) * wins + lax.axis_index("win")
    copies = [
        pltpu.make_async_copy(records.at[s], held.at[s], sem.at[s]) for s in range(segments)
    ]
    for copy in copies:
        copy.start()
    fill_forward_table(table)

    def whitened(s, block):
        rows = held[s, pl.ds(block * BLOCK, BLOCK), :]
        spectra = jnp.dot(rows, table[...], preferred_element_type=jnp.float32)
        real_part, imag_part = spectra[:, :F], spectra[:, F:]
        power = real_part * real_part + imag_part * imag_part
        level = jnp.mean(power, axis=-1, keepdims=True)
        scale = lax.rsqrt(power + 0.1 * level + 1e-06)
        return jnp.concatenate([real_part * scale, imag_part * scale], axis=1)

    halves = near // 2

    def place(number):
        half, core, win = number // (2 * wins), number // wins % 2, number % wins
        return (core * halves + half) * wins + win

    together = max(2, 16 // width)
    for s in range(0, segments, together):
        for k in range(together):
            copies[s + k].wait()
        for block in range(blocks):
            values = [whitened(s + k, block) for k in range(together)]
            for part in range(cut):
                tile = [v[part * width : (part + 1) * width] for v in values]
                tile = jnp.concatenate(tile, axis=0) if together > 1 else tile[0]
                spot = pl.ds((block * segments + s) * width, together * width)
                number = place(jnp.bitwise_xor(mine, part)) if cut > 1 else 0
                out_ref[number, spot, :] = tile.astype(jnp.bfloat16)


def whitened_parts(records, near, wins):
    segments, channels, length = records.shape
    blocks, parts = channels // BLOCK, near * wins
    width = BLOCK // parts
    packed = width % 8 == 0
    cut = parts if packed else 1
    rows = blocks * segments * BLOCK // cut
    hbm = pl.BlockSpec(memory_space=pl.ANY)
    out = pl.pallas_call(
        functools.partial(spectra_kernel, near, wins),
        in_specs=[hbm],
        out_specs=pl.BlockSpec(memory_space=pltpu.VMEM),
        out_shape=jax.ShapeDtypeStruct((cut, rows, 2 * F), jnp.bfloat16),
        scratch_shapes=[
            pltpu.VMEM(records.shape, jnp.bfloat16),
            pltpu.VMEM((length, 2 * F), jnp.bfloat16),
            pltpu.SemaphoreType.DMA((segments,)),
        ],
        compiler_params=pltpu.CompilerParams(vmem_limit_bytes=SPECTRA_VMEM),
    )(records)
    if packed:
        return out
    mine = lax.axis_index("chan") % near * wins + lax.axis_index("win")
    split = out.reshape(blocks, segments, parts, width, 2 * F)
    split = split.transpose(2, 0, 1, 3, 4).reshape(parts, rows // parts, 2 * F)
    split = jnp.take(split, jnp.bitwise_xor(mine, jnp.arange(parts)), axis=0)
    split = split.reshape(near // 2, 2, wins * rows // parts, 2 * F).transpose(1, 0, 2, 3)
    return split.reshape(parts, rows // parts, 2 * F)


def gather(moves, held, sem, others=()):
    copies, spot = [], 0
    for k, (ref, first, count) in enumerate(moves):
        copies.append(
            pltpu.make_async_copy(
                ref.at[pl.ds(first, count)], held.at[pl.ds(spot, count)], sem.at[k]
            )
        )
        spot += count
        copies[-1].start()
    for copy in others:
        copy.start()
    for copy in copies:
        copy.wait()


def add_pairs(near, fold, slots_ref, held, tiles, cross, copies):
    slots = (slots_ref.shape[0] - near - 1) // (2 * near + 2)
    together = min(8, slots)

    def one_pair(index):
        first, second = slots_ref[index], slots_ref[near * slots + index]
        spot = pl.ds(pl.multiple_of(index * fold, fold), fold)
        real_sum, imag_sum = None, None
        for tile in tiles:
            a = held[pl.ds(pl.multiple_of(first + tile, 16), 16), :].astype(jnp.float32)
            b = held[pl.ds(pl.multiple_of(second + tile, 16), 16), :].astype(jnp.float32)
            ar, ai, br, bi = a[:, :F], a[:, F:], b[:, :F], b[:, F:]
            real_part, imag_part = ar * br + ai * bi, ar * bi - ai * br
            real_sum = real_part if real_sum is None else real_sum + real_part
            imag_sum = imag_part if imag_sum is None else imag_sum + imag_part
        if fold == 8:
            real_sum = real_sum[:8] + real_sum[8:]
            imag_sum = imag_sum[:8] + imag_sum[8:]
        if copies:
            real_sum += cross[spot, pl.ds(0, F)]
            imag_sum += cross[spot, pl.ds(F, F)]
        cross[spot, pl.ds(0, F)] = real_sum
        cross[spot, pl.ds(F, F)] = imag_sum

    for owner in range(near):
        if copies:
            copies[owner].wait()

        def some_pairs(step, _):
            for k in range(together):
                one_pair(owner * slots + step * together + k)
            return 0

        count = jnp.clip(slots_ref[2 * near * slots + owner], 0, slots)
        lax.fori_loop(0, lax.div(count + (together - 1), together), some_pairs, 0)


def first_kernel(near, fold, size, rows, slots_ref, *refs):
    pieces, (cross, held, sem) = refs[:6], refs[6:]
    part = (near - 2) * size
    moves = []
    for plane in range(3):
        moves += [(pieces[plane], 0, 2 * size), (pieces[3 + plane], 0, part)]
    gather(moves, held, sem)
    add_pairs(near, fold, slots_ref, held, list(range(0, rows, 16)), cross, [])


def last_kernel(near, fold, windows, size, rows, slot_rows, before, table, *refs):
    pieces, (out_ref, held, cross, table_ref, slots_ref, sem) = refs[:6], refs[6:]
    slots_copy = pltpu.make_async_copy(slot_rows, slots_ref, sem.at[7 + near])
    slots_copy.start()
    table_copy = pltpu.make_async_copy(table, table_ref, sem.at[6])
    table_copy.start()
    span = cross.shape[0] // near
    copies = []
    for owner in range(near):
        spot = pl.ds(owner * span, span)
        copies.append(pltpu.make_async_copy(before.at[spot], cross.at[spot], sem.at[7 + owner]))
    part = (near - 2) * size
    moves = []
    for plane in range(3):
        piece, last = pieces[plane], pieces[3 + plane]
        moves += [(piece, part, piece.shape[0] - part), (last, 0, 2 * size)]
    gather(moves, held, sem, copies)
    slots_copy.wait()
    tiles = [w * near * size + r for w in range(windows) for r in range(0, rows, 16)]
    add_pairs(near, fold, slots_ref, held, tiles, cross, copies)
    table_copy.wait()
    mine = lax.rem(lax.axis_index("chan"), near)
    for owner in range(near):
        spectrum = cross[pl.ds(owner * span, span), :]
        high = spectrum.astype(jnp.bfloat16)
        low = (spectrum - high.astype(jnp.float32)).astype(jnp.bfloat16)
        left = jnp.dot(high, table_ref[...], preferred_element_type=jnp.float32)
        right = jnp.dot(low, table_ref[:, :LAGS], preferred_element_type=jnp.float32)
        lagged = left[:, :LAGS] + (left[:, LAGS:] + right)
        lagged = lagged if out_ref.dtype == jnp.float32 else encode(lagged)
        out_ref[jnp.bitwise_xor(owner, mine)] = lagged


def stack_kernel(near, width, scale, slots_ref, *refs):
    codes, (out, held, sem) = refs[:-3], refs[-3:]
    share, parts = held.shape[0], codes[0].shape[0]
    slots = (slots_ref.shape[0] - near - 1) // (2 * near + 2)
    limits = 2 * near * slots + near
    start = lax.axis_index("win") * share
    lag_index = lax.broadcasted_iota(jnp.int32, (parts, width, LAGS), 2)
    together = min(4, share)
    copies = []
    for slot in range(share):
        tile = slot * width // 16 * 16
        at = limits + start + slot
        high = jnp.where(start + slot < slots_ref[limits + 2 * slots], slots_ref[at + slots], 0)
        keep = (lag_index >= slots_ref[at]) & (lag_index < high)
        kept = []
        for code in codes:
            values = code[:, pl.ds(tile, 16), :].astype(jnp.float32)
            values = values[:, slot * width - tile : slot * width - tile + width, :]
            root = lax.rsqrt(lax.rsqrt(jnp.abs(values))) * scale
            root = jnp.where(values < 0, -root, root)
            kept.append(jnp.where(keep & (values != 0), root, 0.0))
        kept = jnp.concatenate(kept, axis=1) if len(kept) > 1 else kept[0]
        held[slot] = kept.reshape(BLOCK, LAGS)
        if slot % together == together - 1:
            spot = pl.ds(slot + 1 - together, together)
            copies.append(pltpu.make_async_copy(held.at[spot], out.at[spot], sem.at[len(copies)]))
            copies[-1].start()
    for copy in copies:
        copy.wait()


def per_device(records, block_pairs, lag_low, lag_high, slot_count):
    segments, channels, length = records.shape
    blocks = channels // BLOCK
    chans, wins = lax.axis_size("chan"), lax.axis_size("win")
    both = ("chan", "win")
    near = REACH // blocks
    parts, halves = near * wins, near // 2
    width = BLOCK // parts
    rows = segments * width
    size = blocks * rows
    slots = block_pairs.shape[0]
    share = slots // wins
    group_total = chans // near
    group, member = lax.axis_index("chan") // near, lax.axis_index("chan") % near

    def partner(block, distance):
        return lax.ppermute(block, both, [(i, i ^ distance) for i in range(chans * wins)])

    def along(block, to):
        route = [(q * near + j, to(q) * near + j) for q in range(group_total) for j in range(near)]
        return lax.ppermute(block, "chan", [r for r in route if 0 <= r[1] < chans])

    def even(block):
        return along(block, lambda q: q ^ 1)

    def odd(block):
        return along(block, lambda q: ((q + 1) ^ 1) - 1)

    def after(block, *others):
        return lax.optimization_barrier((block,) + others)[0]

    near_blocks = jnp.clip(block_pairs.T - (group - 1) * REACH, 0, 3 * REACH - 1)
    note = jnp.pad(near_blocks, ((0, NOTE_ROWS - 2), (0, 2 * F - slots)))
    note = jnp.where(jnp.arange(NOTE_ROWS)[:, None] == 2, slot_count[0], note).astype(jnp.bfloat16)

    split = whitened_parts(records, near, wins)
    split = split.reshape(2, halves, wins, size, 2 * F)
    sent = split[1].reshape(halves * wins * size, 2 * F)
    other = partner(jnp.concatenate([sent, note], axis=0), wins)
    other_note = other[halves * wins * size :]
    other = other[: halves * wins * size].reshape(halves, wins, size, 2 * F)

    order = [(w, h) for w in range(wins) for h in range(halves)]
    own, notes = [], []
    for w, h in order:
        piece = [split[0, h, w], other[h, w]] + ([note, other_note] if w == 0 else [])
        piece = jnp.concatenate(piece, axis=0)
        if (w, h) == order[-1]:
            piece = after(piece, own[2])
        if w or h:
            piece = partner(piece, h * 2 * wins + w)
        if w == 0:
            notes.append(piece[2 * size :].reshape(2, NOTE_ROWS, 2 * F)[:, :3, :slots])
        own.append(piece[: 2 * size])
    rounds = [own[0], jnp.concatenate(own[1:-1], axis=0), own[-1]]
    planes = []
    for k, sent in enumerate(rounds):
        sent = after(sent, planes[0][0], planes[0][2]) if k == 2 else sent
        planes.append([even(sent), sent, odd(sent)])

    notes = jnp.concatenate(notes, axis=0).astype(jnp.int32)
    level, rest = notes[:, :2] // REACH, notes[:, :2] % REACH
    level = jnp.where(group % 2 == 0, 2 - level, level)
    member_block = (jnp.bitwise_xor(rest // blocks, member), rest % blocks)
    counts = notes[:, 2, 0]

    def first_row(windows):
        row = (level * (windows * near) + member_block[0]) * size + member_block[1] * rows
        row = [row[:, 0].reshape(near * slots), row[:, 1].reshape(near * slots)]
        return jnp.concatenate(row + [counts, lag_low, lag_high, slot_count])

    fold = 16 if width % 16 == 0 else 8
    scale = 2.0 ** math.floor(31 - 0.5 * math.log2(F * segments * wins))
    table = inverse_tables(length, scale / math.sqrt(F * segments * wins))
    hbm = pl.BlockSpec(memory_space=pl.ANY)
    smem = pl.BlockSpec(memory_space=pltpu.SMEM)
    vmem = pl.BlockSpec(memory_space=pltpu.VMEM)
    params = pltpu.CompilerParams(vmem_limit_bytes=VMEM_LIMIT)
    cross = jax.ShapeDtypeStruct((near * slots * fold, 2 * F), jnp.float32)
    table_rows, last_rows = first_row(1), first_row(wins - 1)
    before = pl.pallas_call(
        functools.partial(first_kernel, near, fold, size, rows),
        in_specs=[smem] + [hbm] * 6,
        out_specs=vmem,
        out_shape=cross,
        scratch_shapes=[
            pltpu.VMEM((3 * near * size, 2 * F), jnp.bfloat16),
            pltpu.SemaphoreType.DMA((6,)),
        ],
        compiler_params=params,
    )(table_rows, *planes[0], *planes[1])

    groups = [[q * parts + k for k in range(parts)] for q in range(group_total)]
    lagged = pl.pallas_call(
        functools.partial(last_kernel, near, fold, wins - 1, size, rows),
        in_specs=[hbm, hbm, hbm] + [hbm] * 6,
        out_specs=vmem,
        out_shape=jax.ShapeDtypeStruct(
            (near, slots * fold, LAGS), jnp.bfloat16 if fold == width else jnp.float32
        ),
        scratch_shapes=[
            pltpu.VMEM((3 * (wins - 1) * near * size, 2 * F), jnp.bfloat16),
            pltpu.VMEM(cross.shape, jnp.float32),
            pltpu.VMEM(table.shape, table.dtype),
            pltpu.SMEM(last_rows.shape, jnp.int32),
            pltpu.SemaphoreType.DMA((8 + near,)),
        ],
        compiler_params=params,
    )(last_rows, before, table, *planes[1], *planes[2])
    if fold > width:
        lagged = encode(lagged.reshape(near, slots, fold // width, width, LAGS).sum(axis=2))
    lagged = lagged.reshape(parts, share * width, LAGS)
    code = lax.all_to_all(lagged, both, 0, 0, axis_index_groups=groups, tiled=True)

    return pl.pallas_call(
        functools.partial(stack_kernel, near, width, 1.0 / scale),
        in_specs=[smem, vmem],
        out_specs=hbm,
        out_shape=jax.ShapeDtypeStruct((share, BLOCK, LAGS), jnp.float32),
        scratch_shapes=[
            pltpu.VMEM((share, BLOCK, LAGS), jnp.float32),
            pltpu.SemaphoreType.DMA((max(1, share // 4),)),
        ],
        compiler_params=params,
    )(table_rows, code)


def solution(mesh):
    in_specs = (P("win", "chan", None), P("chan", None), P("chan"), P("chan"), P("chan"))
    out_specs = P(("chan", "win"), None, None)
    return jax.shard_map(
        per_device, mesh=mesh, in_specs=in_specs, out_specs=out_specs, check_vma=False
    )
```
